128 devices in a mesh: wide: 16 (over y, x_hi, core), narrow: 8 (over x_lo, z).
Axes of the slice: x: 4 (x_hi: 2, x_lo: 2; x = x_hi * 2 + x_lo), y: 4, z: 4, core: 2. Of those that a mesh axis runs over, the one named last changes fastest.
Arguments:
- layer_input: bfloat16 [512, 18432], P('wide'), may hold values from -4 to 4
- norm_gain: float32 [18432], replicated, may hold values from 0.1 to 1.9
- w_query: bfloat16 [18432, 12288], P('narrow', 'wide'), may hold values from -0.125 to 0.125
- w_keyvalue: bfloat16 [18432, 512], P('narrow', 'wide'), may hold values from -0.046875 to 0.046875
- w_gate: bfloat16 [18432, 36864], P('narrow', 'wide'), may hold values from -0.046875 to 0.046875
- w_up: bfloat16 [18432, 36864], P('narrow', 'wide'), may hold values from -0.046875 to 0.046875
- key_cache: bfloat16 [512, 512, 256], P(('wide', 'narrow')), may hold values from -6 to 6
- value_cache: bfloat16 [512, 512, 256], P(('wide', 'narrow')), may hold values from -6 to 6
- cache_lengths: int32 [512], P(('wide', 'narrow')), may hold values from 1 to 512, as said below
Outputs:
- attended_heads: bfloat16 [512, 12288], P(None, ('wide', 'narrow'))
- hidden_units: bfloat16 [512, 36864], P(None, ('wide', 'narrow'))
The draws below stay inside these ranges and needn't reach their ends.
Inputs may be any that keep to these rules, and one draw needn't show every extreme that they name: `cache_lengths`: some row has all 512 positions filled and some row has one.
All inputs are finite; a program needn't handle non-finite values.
Results may differ from the reference program's by a relative error of at most 0.0097.
Values may be sent and summed in bfloat16 or wider, within the bound.
A program may use at most 128 MiB of HBM per device.

```python
import jax
import jax.numpy as jnp
from jax import lax

D = 18432
HEADS = 48
HEAD_DIM = 256
FF = 36864
CACHE = 512
ROWS = 512


def draw_cache_lengths(key, part):
    key = jax.random.fold_in(key, 7)
    first_key, second_key = jax.random.split(key)
    lengths = jax.random.randint(first_key, (ROWS,), 1, CACHE + 1)
    order = jax.random.permutation(second_key, ROWS)
    lengths = lengths.at[order[0]].set(CACHE)
    lengths = lengths.at[order[1]].set(1)
    return lengths.astype(jnp.int32)


def levels(key, shape, cuts, least, high):
    factor_of = 1.0
    for position, shards_of in cuts:
        heights = jax.random.uniform(jax.random.fold_in(jax.random.fold_in(key, 6), position), (shards_of,), jnp.float32, least / len(cuts), high / len(cuts))
        factor_of = factor_of * jnp.repeat(jnp.exp(heights), shape[position] // shards_of).reshape((-1,) + (1,) * (len(shape) - 1 - position))
    return factor_of


def normal_values(stream_key, shape, scale, reach, cuts=(), kind=jnp.bfloat16):
    gain = levels(stream_key, shape, cuts, -0.22, 0.18) if cuts else 1.0
    drawn = jax.random.normal(stream_key, shape, jnp.float32) * scale * gain
    return jnp.minimum(jnp.maximum(drawn, -reach), reach).astype(kind)


def setup_inputs(seed: int = 0) -> dict:
    seeds = jax.random.split(jax.random.key(seed), 10)
    return {
        "layer_input": normal_values(seeds[0], (ROWS, D), 0.25, 4.0, ((0, 16),)),
        "norm_gain": jnp.clip(1.0 + 0.18 * jax.random.normal(seeds[1], (D,), jnp.float32), 0.1, 1.9),
        "w_query": normal_values(seeds[2], (D, HEADS * HEAD_DIM), (D // 9) ** -0.5, 0.125, ((0, 8), (1, 16))),
        "w_keyvalue": normal_values(seeds[3], (D, 2 * HEAD_DIM), D ** -0.5, 0.046875, ((0, 8), (1, 16))),
        "w_gate": normal_values(seeds[4], (D, FF), D ** -0.5, 0.046875, ((0, 8), (1, 16))),
        "w_up": normal_values(seeds[5], (D, FF), D ** -0.5, 0.046875, ((0, 8), (1, 16))),
        "key_cache": normal_values(seeds[6], (ROWS, CACHE, HEAD_DIM), 1.0, 6.0, ((0, 128),)),
        "value_cache": normal_values(seeds[7], (ROWS, CACHE, HEAD_DIM), 1.0, 6.0, ((0, 128),)),
        "cache_lengths": draw_cache_lengths(jax.random.fold_in(seeds[9], 71), 0),
    }


def row_attention(query, keyvalue, keys, values, length):
    head_dim = keys.shape[1]
    scale = head_dim ** (-0.5)
    heads = query.reshape(-1, head_dim)
    scores = jnp.dot(heads, keys.T, preferred_element_type=jnp.float32) * scale
    valid = jnp.arange(keys.shape[0], dtype=jnp.int32) < length
    raised = jnp.where(valid[None, :], jnp.exp(scores), 0.0)
    own_score = jnp.dot(heads, keyvalue[:head_dim], preferred_element_type=jnp.float32) * scale
    own_weight = jnp.exp(own_score)
    total = lax.optimization_barrier(jnp.sum(raised, axis=1)) + own_weight
    probs = (raised / total[:, None]).astype(jnp.bfloat16)
    own_prob = (own_weight / total).astype(jnp.bfloat16)
    attended = jnp.dot(probs, values, preferred_element_type=jnp.float32)
    attended = attended + own_prob.astype(jnp.float32)[:, None] * keyvalue[head_dim:].astype(jnp.float32)[None, :]
    return attended.astype(jnp.bfloat16).reshape(-1)

def layer_norm(rows, norm_gain):
    values = rows.astype(jnp.float32)
    average = lax.optimization_barrier(jnp.mean(values, axis=1, keepdims=True))
    centred = values - average
    spread = lax.optimization_barrier(jnp.mean(centred * centred, axis=1, keepdims=True))
    return (centred * lax.rsqrt(spread + 1e-05) * norm_gain[None, :]).astype(jnp.bfloat16)

def reference(layer_input, norm_gain, w_query, w_keyvalue, w_gate, w_up, key_cache, value_cache, cache_lengths):
    normed = layer_norm(layer_input, norm_gain)
    query = jnp.dot(normed, w_query, preferred_element_type=jnp.float32).astype(jnp.bfloat16)
    keyvalue = jnp.dot(normed, w_keyvalue, preferred_element_type=jnp.float32).astype(jnp.bfloat16)
    gate = jnp.dot(normed, w_gate, preferred_element_type=jnp.float32)
    upper = jnp.dot(normed, w_up, preferred_element_type=jnp.float32)
    hidden = (jax.nn.silu(gate) * upper).astype(jnp.bfloat16)

    def one_row(packed):
        return row_attention(packed[0], packed[1], packed[2], packed[3], packed[4])
    attended = lax.map(one_row, (query, keyvalue, key_cache, value_cache, cache_lengths))
    return (attended, hidden)
```

```python
import functools

import jax
import jax.numpy as jnp
from jax import lax
from jax.experimental import pallas as pl
from jax.experimental.pallas import tpu as pltpu
from jax.sharding import PartitionSpec as P

MESH = pl.DeviceIdType.MESH
F32 = jnp.float32
BF16 = jnp.bfloat16
UNITS = 8
LANES = 128
Q_SPLIT = (16, 16, 16, 8)
H_SPLIT = (80, 80, 64, 64)
MESSAGES = 10


def sum_scratch(split, dtype):
    a, b, xa, xb = split
    ab, xr = a + b, xa + xb
    n = UNITS
    return [
        pltpu.VMEM((n, 2, 4 * ab, LANES), dtype),
        pltpu.VMEM((n, 2, ab, LANES), dtype),
        pltpu.VMEM((n, 2, ab, LANES), dtype),
        pltpu.VMEM((n, 2, a, LANES), dtype),
        pltpu.VMEM((n, 2, b, LANES), dtype),
        pltpu.VMEM((n, 2, ab, LANES), dtype),
        pltpu.VMEM((n, ab, LANES), dtype),
        pltpu.VMEM((n, 2, 4, xr, LANES), dtype),
        pltpu.VMEM((n, 4, xr, LANES), dtype),
        pltpu.VMEM((n, 4 * xr, LANES), dtype),
        pltpu.VMEM((n, xr, LANES), dtype),
        pltpu.VMEM((n, xr, LANES), dtype),
        pltpu.VMEM((n, xa, LANES), dtype),
        pltpu.VMEM((n, xb, LANES), dtype),
        pltpu.SemaphoreType.DMA((n, MESSAGES)),
        pltpu.SemaphoreType.DMA((n, MESSAGES)),
    ]


class Summer:
    def __init__(self, split, dtype, refs, here, up, down, across):
        self.split, self.dtype = split, dtype
        (
            self.zbuf, self.z_up1, self.z_dn1, self.z_up2, self.z_dn2, self.fin, self.x_last,
            self.cbuf, self.c_in, self.xz, self.x_up1, self.x_dn1, self.x_up2, self.x_dn2,
            self.send, self.recv,
        ) = refs
        self.x, self.z = here
        self.up, self.down, self.across = up, down, across
        self.align = 16 if dtype == BF16 else 8

    def copy(self, k, t):
        a, b, xa, xb = self.split
        ab, xr = a + b, xa + xb
        src, dst, to = [
            (self.zbuf.at[t, :, 0:ab], self.z_up1.at[t], self.up),
            (self.zbuf.at[t, :, ab : 2 * ab], self.z_dn1.at[t], self.down),
            (self.cbuf.at[t, 1], self.c_in.at[t], self.across),
            (self.zbuf.at[t, :, 2 * ab : 2 * ab + a], self.z_up2.at[t], self.up),
            (self.zbuf.at[t, :, 2 * ab + a : 3 * ab], self.z_dn2.at[t], self.down),
            (self.xz.at[t, 0:xr], self.x_up1.at[t], self.up),
            (self.xz.at[t, xr : 2 * xr], self.x_dn1.at[t], self.down),
            (self.fin.at[t, 1], self.x_last.at[t], self.across),
            (self.xz.at[t, 2 * xr : 2 * xr + xa], self.x_up2.at[t], self.up),
            (self.xz.at[t, 2 * xr + xa : 3 * xr], self.x_dn2.at[t], self.down),
        ][k]
        return pltpu.make_async_remote_copy(
            src_ref=src, dst_ref=dst, send_sem=self.send.at[t, k], recv_sem=self.recv.at[t, k],
            device_id=to, device_id_type=MESH,
        )

    def places(self, a, b, z_to):
        dz = lax.rem(z_to - self.z + 4, 4)
        ab = a + b
        first = jnp.where(dz == 0, 3 * ab, jnp.where(dz == 1, 2 * ab, jnp.where(dz == 2, 0, a + 2 * b)))
        second = jnp.where(
            dz == 0, 3 * ab + a, jnp.where(dz == 1, a, jnp.where(dz == 2, ab, 2 * ab + a))
        )
        return first, second

    def at(self, start, size):
        return pl.ds(pl.multiple_of(start, self.align), size)

    def start_first(self, t):
        for k in (0, 1, 2):
            self.copy(k, t).start()

    def second(self, t):
        a, b, xa, xb = self.split
        ab, xr = a + b, xa + xb
        self.copy(0, t).wait_recv()
        for i in (0, 1):
            self.zbuf[t, i, 2 * ab : 2 * ab + a] = (
                self.zbuf[t, i, 2 * ab : 2 * ab + a].astype(F32) + self.z_up1[t, i, 0:a].astype(F32)
            ).astype(self.dtype)
        self.copy(3, t).start()
        self.copy(1, t).wait_recv()
        for i in (0, 1):
            self.zbuf[t, i, 2 * ab + a : 3 * ab] = (
                self.zbuf[t, i, 2 * ab + a : 3 * ab].astype(F32) + self.z_dn1[t, i, 0:b].astype(F32)
            ).astype(self.dtype)
        self.copy(4, t).start()
        self.copy(2, t).wait_recv()
        for z_to in range(4):
            first, second = self.places(xa, xb, z_to)
            both = (
                self.cbuf[t, 0, z_to].astype(F32) + self.c_in[t, z_to].astype(F32)
            ).astype(self.dtype)
            self.xz[t, self.at(first, xa)] = both[0:xa]
            self.xz[t, self.at(second, xb)] = both[xa:xr]
        self.copy(5, t).start()
        self.copy(6, t).start()

    def third(self, t):
        a, b, xa, xb = self.split
        ab, xr = a + b, xa + xb
        self.copy(3, t).wait_recv()
        self.copy(4, t).wait_recv()
        for i in (0, 1):
            place = jnp.where(self.x == i, 0, 1)
            self.fin[t, place, 0:a] = (
                self.zbuf[t, i, 3 * ab : 3 * ab + a].astype(F32)
                + self.z_up2[t, i].astype(F32)
                + self.z_dn1[t, i, b:ab].astype(F32)
            ).astype(self.dtype)
            self.fin[t, place, a:ab] = (
                self.zbuf[t, i, 3 * ab + a : 4 * ab].astype(F32)
                + self.z_dn2[t, i].astype(F32)
                + self.z_up1[t, i, a:ab].astype(F32)
            ).astype(self.dtype)
        self.copy(7, t).start()
        self.copy(5, t).wait_recv()
        self.xz[t, 2 * xr : 2 * xr + xa] = (
            self.xz[t, 2 * xr : 2 * xr + xa].astype(F32) + self.x_up1[t, 0:xa].astype(F32)
        ).astype(self.dtype)
        self.copy(8, t).start()
        self.copy(6, t).wait_recv()
        self.xz[t, 2 * xr + xa : 3 * xr] = (
            self.xz[t, 2 * xr + xa : 3 * xr].astype(F32) + self.x_dn1[t, 0:xb].astype(F32)
        ).astype(self.dtype)
        self.copy(9, t).start()

    def last(self, t):
        a, b, xa, xb = self.split
        ab, xr = a + b, xa + xb
        self.copy(7, t).wait_recv()
        one = self.fin[t, 0].astype(F32) + self.x_last[t].astype(F32)
        self.copy(8, t).wait_recv()
        self.copy(9, t).wait_recv()
        two = (
            self.xz[t, 3 * xr : 3 * xr + xa].astype(F32)
            + self.x_up2[t].astype(F32)
            + self.x_dn1[t, xb:xr].astype(F32)
        )
        three = (
            self.xz[t, 3 * xr + xa : 4 * xr].astype(F32)
            + self.x_dn2[t].astype(F32)
            + self.x_up1[t, xa:xr].astype(F32)
        )
        return one, two, three

    def finish(self, t):
        for k in range(MESSAGES):
            self.copy(k, t).wait_send()


def kernel(
    x_hbm, gain_hbm, wq_hbm, wkv_hbm, wg_hbm, wu_hbm, k_hbm, v_hbm, len_ref,
    att_ref, hid_ref,
    xbuf, gain, wq, wkv, wg, wu, keys, values, load_sem,
    piece, pbuf, ag_send, ag_recv, ag_side,
    qtmp, gtmp, utmp,
    qout, qin, q_send, q_recv,
    att1, att1_in, att1_send, att1_recv,
    att2, att2_in, att2_send, att2_recv,
    *sum_refs,
):
    w = lax.axis_index("wide")
    n = lax.axis_index("narrow")
    y, h, c = w // 4, lax.rem(w // 2, 2), lax.rem(w, 2)
    x, z = n // 4, lax.rem(n, 4)
    slab = piece.shape[3]
    tiles = slab // LANES
    rows = xbuf.shape[0]
    width = xbuf.shape[1]

    def wide(yy, hh, cc):
        return (yy * 2 + hh) * 2 + cc

    y_up = (wide(lax.rem(y + 1, 4), h, c), n)
    y_down = (wide(lax.rem(y + 3, 4), h, c), n)
    side = (wide(y, h, 1 - c), n)
    pair = (wide(y, 1 - h, c), (1 - x) * 4 + z)
    z_up = (w, x * 4 + lax.rem(z + 1, 4))
    z_down = (w, x * 4 + lax.rem(z + 3, 4))
    across = (w, (1 - x) * 4 + z)

    loads = [
        pltpu.make_async_copy(src, dst, load_sem.at[i])
        for i, (src, dst) in enumerate(
            [
                (x_hbm, xbuf), (gain_hbm, gain), (wq_hbm, wq), (wkv_hbm, wkv),
                (wg_hbm, wg), (wu_hbm, wu), (k_hbm, keys), (v_hbm, values),
            ]
        )
    ]
    for load in loads:
        load.start()

    barrier = pltpu.get_barrier_semaphore()
    for s in range(1, 16):
        pl.semaphore_signal(barrier, inc=1, device_id=(lax.rem(w + s, 16), n), device_id_type=MESH)
    for s in range(1, 8):
        pl.semaphore_signal(barrier, inc=1, device_id=(w, lax.rem(n + s, 8)), device_id_type=MESH)
    pl.semaphore_signal(barrier, inc=1, device_id=pair, device_id_type=MESH)

    loads[0].wait()
    loads[1].wait()
    step_cols = 1024

    def add_block(i, total):
        block = xbuf[:, pl.ds(pl.multiple_of(i * step_cols, step_cols), step_cols)].astype(F32)
        for s in range(step_cols // 256):
            total = total + block[:, s * 256 : (s + 1) * 256]
        return total

    zero = jnp.zeros((rows, 256), F32)
    total = lax.fori_loop(0, width // step_cols, add_block, zero)
    average = jnp.sum(total, axis=1, keepdims=True) * (1.0 / width)

    def add_square(i, total):
        block = xbuf[:, pl.ds(pl.multiple_of(i * step_cols, step_cols), step_cols)].astype(F32)
        block = block - average
        block = block * block
        for s in range(step_cols // 256):
            total = total + block[:, s * 256 : (s + 1) * 256]
        return total

    total = lax.fori_loop(0, width // step_cols, add_square, zero)
    spread = jnp.sum(total, axis=1, keepdims=True) * (1.0 / width)
    factor = lax.rsqrt(spread + 1e-05)

    def normed(owner, i):
        start = pl.multiple_of(owner * slab + i * LANES, LANES)
        block = xbuf[:, pl.ds(start, LANES)].astype(F32)
        return ((block - average) * factor * gain[pl.ds(owner * tiles + i, 1), :]).astype(BF16)

    pair_n = (1 - x) * 4 + z
    for i in range(tiles):
        pbuf[:, i * LANES : (i + 1) * LANES] = normed(pair_n, i)
    for i in range(tiles):
        piece[0, c, :, i * LANES : (i + 1) * LANES] = normed(n, i)

    pl.semaphore_wait(barrier, 23)

    def gather_copy(k):
        src, slot, to = [
            (pbuf, 1, pair),
            (piece.at[0, c], 2, y_up),
            (piece.at[0, c], 3, y_down),
            (piece.at[1, c], 4, y_up),
            (piece.at[1, c], 5, y_down),
            (piece.at[2, c], 6, y_up),
            (piece.at[5, c], 7, y_down),
        ][k]
        return pltpu.make_async_remote_copy(
            src_ref=src, dst_ref=piece.at[slot, c], send_sem=ag_send.at[k], recv_sem=ag_recv.at[k],
            device_id=to, device_id_type=MESH,
        )

    def side_copy(t):
        return pltpu.make_async_remote_copy(
            src_ref=piece.at[t, c], dst_ref=piece.at[t, c], send_sem=ag_send.at[7 + t],
            recv_sem=ag_side.at[t], device_id=side, device_id_type=MESH,
        )

    def side_wait(t):
        pltpu.make_async_remote_copy(
            src_ref=piece.at[t, 1 - c], dst_ref=piece.at[t, 1 - c], send_sem=ag_send.at[7 + t],
            recv_sem=ag_side.at[t], device_id=side, device_id_type=MESH,
        ).wait_recv()

    for k in (0, 1, 2):
        gather_copy(k).start()
    side_copy(0).start()

    count = len(sum_refs) // 2
    q_sum = Summer(Q_SPLIT, F32, sum_refs[:count], (x, z), z_up, z_down, across)
    h_sum = Summer(H_SPLIT, BF16, sum_refs[count:], (x, z), z_up, z_down, across)

    def chip_of(t):
        group, odd = t // 2, lax.rem(t, 2)
        dy = jnp.where(group == 0, 0, jnp.where(group == 3, 2, jnp.where(odd == 0, 3, 1)))
        flip = jnp.where((group == 0) | (group == 3), odd, group - 1)
        return lax.rem(y + dy, 4), lax.rem(h + flip, 2)

    def project_q(t):
        side_wait(t)
        piece_t = piece[t].reshape(2 * rows, slab)
        for s in range(3):
            qtmp[:, s * 256 : (s + 1) * 256] = jnp.dot(
                piece_t, wq[:, s * 256 : (s + 1) * 256], preferred_element_type=F32
            )
        qtmp[:, 768:896] = jnp.zeros((2 * rows, LANES), F32)
        qtmp[:, 768:800] = jnp.dot(piece_t, wkv[...], preferred_element_type=F32)
        qtmp[:, 768:896] = pltpu.roll(qtmp[:, 768:896], 32 * lax.rem(w, 4), axis=1)
        low = lax.broadcasted_iota(jnp.int32, (8, 896), 0) < 4
        for m in range(4):
            top = qtmp[8 * m : 8 * m + 8, :]
            bottom = qtmp[rows + 8 * m : rows + 8 * m + 8, :]
            even = jnp.where(low, top, pltpu.roll(bottom, 4, axis=0))
            odd = jnp.where(low, pltpu.roll(top, 4, axis=0), bottom)
            for to, block in ((2 * m, even), (2 * m + 1, odd)):
                x_to, z_to = to // 4, to % 4
                first, second = q_sum.places(16, 16, z_to)
                far = jnp.where(x == x_to, 0, 1)
                for s in range(2):
                    q_sum.zbuf[t, x_to, q_sum.at(first + 8 * s, 8)] = block[:, s * 128 : (s + 1) * 128]
                    q_sum.zbuf[t, x_to, q_sum.at(second + 8 * s, 8)] = block[
                        :, (2 + s) * 128 : (3 + s) * 128
                    ]
                for s in range(3):
                    q_sum.cbuf[t, far, z_to, 8 * s : 8 * s + 8] = block[:, (4 + s) * 128 : (5 + s) * 128]
        q_sum.start_first(t)

    def project_h(t):
        piece_t = piece[t].reshape(2 * rows, slab)
        for s in range(gtmp.shape[1] // 256):
            cols = slice(s * 256, (s + 1) * 256)
            gtmp[:, cols] = jnp.dot(piece_t, wg[:, cols], preferred_element_type=F32).astype(BF16)
            utmp[:, cols] = jnp.dot(piece_t, wu[:, cols], preferred_element_type=F32).astype(BF16)
        for to in range(8):
            x_to, z_to = to // 4, to % 4
            first, second = h_sum.places(80, 80, z_to)
            far = jnp.where(x == x_to, 0, 1)
            start = 288 * to
            base = start // LANES * LANES
            stop = min(-(-(start + 288) // LANES) * LANES, gtmp.shape[1])
            off = start - base
            g = gtmp[:, base:stop]
            u = utmp[:, base:stop]
            g0, g1, gr = g[:, off : off + 128], g[:, off + 128 : off + 256], g[:, off + 256 : off + 288]
            u0, u1, ur = u[:, off : off + 128], u[:, off + 128 : off + 256], u[:, off + 256 : off + 288]
            h_sum.zbuf[t, x_to, h_sum.at(first, 64)] = g0
            h_sum.zbuf[t, x_to, h_sum.at(first + 64, 16)] = g1[0:16]
            h_sum.zbuf[t, x_to, h_sum.at(second, 48)] = g1[16:64]
            h_sum.zbuf[t, x_to, h_sum.at(second + 48, 32)] = u0[0:32]
            h_sum.cbuf[t, far, z_to, 0:32] = u0[32:64]
            h_sum.cbuf[t, far, z_to, 32:96] = u1
            h_sum.cbuf[t, far, z_to, 96:128, 0:32] = gr[0:32]
            h_sum.cbuf[t, far, z_to, 96:128, 32:64] = ur[0:32]
            h_sum.cbuf[t, far, z_to, 96:128, 64:96] = gr[32:64]
            h_sum.cbuf[t, far, z_to, 96:128, 96:128] = ur[32:64]
        h_sum.start_first(t)

    def q_copy(t, core):
        yy, hh = chip_of(t)
        to = wide(yy, hh, core)
        return to, pltpu.make_async_remote_copy(
            src_ref=qout.at[t, core], dst_ref=qin.at[w], send_sem=q_send.at[t, core],
            recv_sem=q_recv.at[w], device_id=(to, n), device_id_type=MESH,
        )

    def finish_q(t):
        one, two, three = q_sum.last(t)
        blocks = [one[8 * s : 8 * s + 8] for s in range(4)]
        blocks += [two[0:8], two[8:16], three]
        blocks = [block.astype(BF16).astype(F32) for block in blocks]
        for core in range(2):
            for s, block in enumerate(blocks):
                qout[t, core, :, s * 128 : (s + 1) * 128] = block[4 * core : 4 * core + 4]
            to, copy = q_copy(t, core)

            @pl.when(to != w)
            def _():
                copy.start()

            @pl.when(to == w)
            def _():
                for s, block in enumerate(blocks):
                    qin[w, :, s * 128 : (s + 1) * 128] = block[4 * core : 4 * core + 4]

    def silu(v):
        return v / (1.0 + jnp.exp(-v))

    def finish_h(t):
        one, two, three = h_sum.last(t)
        yy, hh = chip_of(t)
        start = (yy * 2 + hh) * 64

        def out_rows(offset, size):
            return pl.ds(pl.multiple_of(start + offset, 32), size)

        hid_ref[out_rows(0, 32), 0:128] = (silu(one[0:32]) * one[128:160]).astype(BF16)
        hid_ref[out_rows(32, 32), 0:128] = (silu(one[32:64]) * two[0:32]).astype(BF16)
        hid_ref[out_rows(0, 32), 128:256] = (silu(one[64:96]) * two[32:64]).astype(BF16)
        hid_ref[out_rows(32, 32), 128:256] = (silu(one[96:128]) * three[0:32]).astype(BF16)
        rest = three[32:64]
        rest = silu(rest) * pltpu.roll(rest, 96, axis=1)
        hid_ref[out_rows(0, 32), 256:288] = rest[:, 0:32].astype(BF16)
        hid_ref[out_rows(32, 32), 256:288] = pltpu.roll(rest, 64, axis=1)[:, 0:32].astype(BF16)

    def att1_copy(s):
        to = lax.rem(n + s, 8)
        return pltpu.make_async_remote_copy(
            src_ref=att1.at[to], dst_ref=att1_in.at[n], send_sem=att1_send.at[s],
            recv_sem=att1_recv.at[s], device_id=(w, to), device_id_type=MESH,
        )

    def att2_copy(s):
        to = lax.rem(w + s, 16)
        return pltpu.make_async_remote_copy(
            src_ref=att2.at[to], dst_ref=att2_in.at[w], send_sem=att2_send.at[s],
            recv_sem=att2_recv.at[s], device_id=(to, n), device_id_type=MESH,
        )

    def attend():
        loads[6].wait()
        loads[7].wait()

        @pl.loop(1, 16)
        def _(s):
            source = lax.rem(w + s, 16)
            pltpu.make_async_remote_copy(
                src_ref=qin.at[source], dst_ref=qin.at[source], send_sem=q_send.at[0, 0],
                recv_sem=q_recv.at[source], device_id=side, device_id_type=MESH,
            ).wait_recv()

        scale = 256 ** (-0.5)
        for r in range(4):
            heads = jnp.concatenate(
                [qin[:, r, s * 256 : (s + 1) * 256] for s in range(3)], axis=0
            )
            kv = qin[:, r, 768:896]
            kv = [jnp.sum(kv[4 * i : 4 * i + 4], axis=0, keepdims=True) for i in range(4)]
            own_key = jnp.concatenate(kv[0:2], axis=1)
            own_value = jnp.concatenate(kv[2:4], axis=1)
            scores = lax.dot_general(
                heads.astype(BF16), keys[r], (((1,), (1,)), ((), ())), preferred_element_type=F32
            ) * scale
            valid = lax.broadcasted_iota(jnp.int32, scores.shape, 1) < len_ref[r]
            raised = jnp.where(valid, jnp.exp(scores), 0.0)
            own = jnp.exp(jnp.sum(heads * own_key, axis=1, keepdims=True) * scale)
            total = jnp.sum(raised, axis=1, keepdims=True) + own
            probs = (raised / total).astype(BF16)
            own_prob = (own / total).astype(BF16).astype(F32)
            out = jnp.dot(probs, values[r], preferred_element_type=F32) + own_prob * own_value
            flat = jnp.concatenate(
                [out[0:16], out[16:32], out[32:48], jnp.zeros((16, LANES), F32)], axis=1
            )
            for to in range(8):
                att1[to, r] = flat[:, 96 * to : 96 * to + 128].astype(BF16)
        att1_in[n] = att1[n]
        for s in range(1, 8):
            att1_copy(s).start()

    def spread_heads():
        for s in range(1, 8):
            source = lax.rem(n + 8 - s, 8)
            pltpu.make_async_remote_copy(
                src_ref=att1.at[source], dst_ref=att1_in.at[source], send_sem=att1_send.at[s],
                recv_sem=att1_recv.at[s], device_id=(w, source), device_id_type=MESH,
            ).wait_recv()
        att2[...] = jnp.swapaxes(att1_in[...].reshape(32, 16, LANES), 0, 1)
        att2_in[w] = att2[w]
        for s in range(1, 16):
            att2_copy(s).start()

    def gather_heads():
        for s in range(1, 16):
            source = lax.rem(w + 16 - s, 16)
            pltpu.make_async_remote_copy(
                src_ref=att2.at[source], dst_ref=att2_in.at[source], send_sem=att2_send.at[s],
                recv_sem=att2_recv.at[s], device_id=(source, n), device_id_type=MESH,
            ).wait_recv()
        att_ref[...] = att2_in[...].reshape(512, LANES)[:, 0:96]

    def unit(j):
        is_q = (j < 6) | (j == 7) | (j == 8)
        t = jnp.where(j < 6, j, jnp.where(is_q, j - 1, jnp.where(j == 6, 0, j - 8)))
        return is_q, t

    def stage(j, q_step, h_step):
        real = (j >= 0) & (j < 16)
        is_q, t = unit(j)

        @pl.when(real & is_q)
        def _():
            q_step(t)

        @pl.when(real & jnp.logical_not(is_q))
        def _():
            h_step(t)

    loads[2].wait()
    loads[3].wait()

    @pl.loop(0, 19)
    def _(j):
        @pl.when(j == 6)
        def _():
            loads[4].wait()
            loads[5].wait()

        stage(j, project_q, project_h)

        @pl.when(j == 0)
        def _():
            gather_copy(0).wait_recv()
            side_copy(1).start()
            gather_copy(3).start()
            gather_copy(4).start()
            gather_copy(1).wait_recv()
            side_copy(2).start()
            gather_copy(5).start()
            gather_copy(2).wait_recv()
            side_copy(3).start()

        @pl.when(j == 3)
        def _():
            gather_copy(4).wait_recv()
            side_copy(5).start()
            gather_copy(6).start()
            gather_copy(3).wait_recv()
            side_copy(4).start()

        @pl.when(j == 6)
        def _():
            gather_copy(5).wait_recv()
            side_copy(6).start()
            gather_copy(6).wait_recv()
            side_copy(7).start()

        stage(j - 1, q_sum.second, h_sum.second)
        stage(j - 2, q_sum.third, h_sum.third)
        stage(j - 3, finish_q, finish_h)

        @pl.when(j == 13)
        def _():
            attend()

        @pl.when(j == 15)
        def _():
            spread_heads()

    gather_heads()

    for k in range(7):
        gather_copy(k).wait_send()
    for t in range(8):
        side_copy(t).wait_send()

    @pl.loop(0, 8)
    def _(t):
        q_sum.finish(t)
        h_sum.finish(t)
        for core in range(2):
            to, copy = q_copy(t, core)

            @pl.when(to != w)
            def _():
                copy.wait_send()

    for s in range(1, 8):
        att1_copy(s).wait_send()
    for s in range(1, 16):
        att2_copy(s).wait_send()


def body(
    layer_input, norm_gain, w_query, w_keyvalue, w_gate, w_up, key_cache, value_cache, cache_lengths
):
    rows, width = layer_input.shape
    slab = w_query.shape[0]
    anywhere = pl.BlockSpec(memory_space=pl.ANY)
    vmem = pl.BlockSpec(memory_space=pltpu.VMEM)
    dma = pltpu.SemaphoreType.DMA
    attended, hidden = pl.pallas_call(
        kernel,
        out_shape=(
            jax.ShapeDtypeStruct((512, 96), BF16),
            jax.ShapeDtypeStruct((512, 288), BF16),
        ),
        in_specs=[anywhere] * 8 + [pl.BlockSpec(memory_space=pltpu.SMEM)],
        out_specs=(vmem, vmem),
        scratch_shapes=[
            pltpu.VMEM((rows, width), BF16),
            pltpu.VMEM((width // LANES, LANES), F32),
            pltpu.VMEM(w_query.shape, BF16),
            pltpu.VMEM(w_keyvalue.shape, BF16),
            pltpu.VMEM(w_gate.shape, BF16),
            pltpu.VMEM(w_up.shape, BF16),
            pltpu.VMEM(key_cache.shape, BF16),
            pltpu.VMEM(value_cache.shape, BF16),
            dma((8,)),
            pltpu.VMEM((UNITS, 2, rows, slab), BF16),
            pltpu.VMEM((rows, slab), BF16),
            dma((15,)),
            dma((7,)),
            dma((8,)),
            pltpu.VMEM((2 * rows, 896), F32),
            pltpu.VMEM((2 * rows, w_gate.shape[1]), BF16),
            pltpu.VMEM((2 * rows, w_up.shape[1]), BF16),
            pltpu.VMEM((UNITS, 2, 4, 896), F32),
            pltpu.VMEM((16, 4, 896), F32),
            dma((UNITS, 2)),
            dma((16,)),
            pltpu.VMEM((8, 4, 16, LANES), BF16),
            pltpu.VMEM((8, 4, 16, LANES), BF16),
            dma((8,)),
            dma((8,)),
            pltpu.VMEM((16, 32, LANES), BF16),
            pltpu.VMEM((16, 32, LANES), BF16),
            dma((16,)),
            dma((16,)),
        ]
        + sum_scratch(Q_SPLIT, F32)
        + sum_scratch(H_SPLIT, BF16),
        compiler_params=pltpu.CompilerParams(
            collective_id=0, has_side_effects=True, vmem_limit_bytes=60 * 1024 * 1024
        ),
    )(
        layer_input, norm_gain.reshape(width // LANES, LANES), w_query, w_keyvalue, w_gate, w_up,
        key_cache, value_cache, cache_lengths,
    )
    return attended, hidden


def solution(mesh):
    placed = (
        P("wide", None),
        P(),
        P("narrow", "wide"),
        P("narrow", "wide"),
        P("narrow", "wide"),
        P("narrow", "wide"),
        P(("wide", "narrow"), None, None),
        P(("wide", "narrow"), None, None),
        P(("wide", "narrow")),
    )
    return jax.shard_map(
        body,
        mesh=mesh,
        in_specs=placed,
        out_specs=(P(None, ("wide", "narrow")), P(None, ("wide", "narrow"))),
        check_vma=False,
    )
```

```python
import functools

import jax
import jax.numpy as jnp
from jax import lax
from jax.experimental import pallas as pl
from jax.experimental.pallas import tpu as pltpu
from jax.sharding import PartitionSpec as P

MESH = pl.DeviceIdType.MESH
F32 = jnp.float32
BF16 = jnp.bfloat16
UNITS = 8
LANES = 128
Q_SPLIT = (16, 16, 16, 8)
H_SPLIT = (80, 80, 64, 64)
MESSAGES = 10
PARTS = 3
GATHER = {
    1: (1, 1), 2: (2, 2), 4: (5, 1), 5: (4, 1), 6: (6, 1), 8: (7, 1),
}
Q_PROJECT = {
    0: (0, 1), 2: (1, 1), 3: (2, 2), 8: (4, 2), 9: (6, 2),
}
H_PROJECT = {
    4: (0, 2), 9: (6, 2), 15: (4, 2), 18: (2, 2),
}
Q_SECOND = {
    1: (0, 1), 6: (1, 1), 7: (3, 1), 8: (2, 1), 12: (5, 1), 13: (4, 1), 14: (6, 2),
}
Q_THIRD = {
    3: (0, 1), 10: (3, 1), 11: (2, 1), 12: (1, 1), 16: (4, 1), 17: (5, 3),
}
H_SECOND = {
    9: (0, 1), 16: (1, 1), 17: (6, 2), 23: (4, 2), 24: (3, 1), 25: (2, 1),
}
H_THIRD = {
    23: (6, 1), 25: (7, 1), 26: (0, 1), 27: (4, 2), 28: (3, 1), 29: (1, 1), 30: (2, 1),
}
Q_LAST = {
    15: (3, 1), 16: (1, 1), 18: (4, 1), 19: (0, 1), 20: (7, 1), 21: (5, 2), 22: (2, 1),
}
H_LAST = {
    30: (6, 2), 31: (0, 1), 32: (4, 2), 33: (3, 1), 34: (1, 2),
}
ATTEND = 23
SPREAD = 29
PASSES = 35


def sum_scratch(split, dtype):
    a, b, xa, xb = split
    ab, xr = a + b, xa + xb
    n = UNITS
    return [
        pltpu.VMEM((n, 2, 4 * ab, LANES), dtype),
        pltpu.VMEM((n, 2, ab, LANES), dtype),
        pltpu.VMEM((n, 2, ab, LANES), dtype),
        pltpu.VMEM((n, 2, a, LANES), dtype),
        pltpu.VMEM((n, 2, b, LANES), dtype),
        pltpu.VMEM((n, 2, ab, LANES), dtype),
        pltpu.VMEM((n, ab, LANES), dtype),
        pltpu.VMEM((n, 2, 4, xr, LANES), dtype),
        pltpu.VMEM((n, 4, xr, LANES), dtype),
        pltpu.VMEM((n, 4 * xr, LANES), dtype),
        pltpu.VMEM((n, xr, LANES), dtype),
        pltpu.VMEM((n, xr, LANES), dtype),
        pltpu.VMEM((n, xa, LANES), dtype),
        pltpu.VMEM((n, xb, LANES), dtype),
        pltpu.SemaphoreType.DMA((MESSAGES,)),
        pltpu.SemaphoreType.DMA((n, MESSAGES)),
    ]


class Summer:
    def __init__(self, split, dtype, refs, here, up, down, across):
        self.split, self.dtype = split, dtype
        (
            self.zbuf, self.z_up1, self.z_dn1, self.z_up2, self.z_dn2, self.fin, self.x_last,
            self.cbuf, self.c_in, self.xz, self.x_up1, self.x_dn1, self.x_up2, self.x_dn2,
            self.send, self.recv,
        ) = refs
        self.x, self.z = here
        self.up, self.down, self.across = up, down, across
        self.align = 16 if dtype == BF16 else 8

    def copy(self, k, t):
        a, b, xa, xb = self.split
        ab, xr = a + b, xa + xb
        src, dst, to = [
            (self.zbuf.at[t, :, 0:ab], self.z_up1.at[t], self.up),
            (self.zbuf.at[t, :, ab : 2 * ab], self.z_dn1.at[t], self.down),
            (self.cbuf.at[t, 1], self.c_in.at[t], self.across),
            (self.zbuf.at[t, :, 2 * ab : 2 * ab + a], self.z_up2.at[t], self.up),
            (self.zbuf.at[t, :, 2 * ab + a : 3 * ab], self.z_dn2.at[t], self.down),
            (self.xz.at[t, 0:xr], self.x_up1.at[t], self.up),
            (self.xz.at[t, xr : 2 * xr], self.x_dn1.at[t], self.down),
            (self.fin.at[t, 1], self.x_last.at[t], self.across),
            (self.xz.at[t, 2 * xr : 2 * xr + xa], self.x_up2.at[t], self.up),
            (self.xz.at[t, 2 * xr + xa : 3 * xr], self.x_dn2.at[t], self.down),
        ][k]
        return pltpu.make_async_remote_copy(
            src_ref=src, dst_ref=dst, send_sem=self.send.at[k], recv_sem=self.recv.at[0 if isinstance(t, slice) else t, k],
            device_id=to, device_id_type=MESH,
        )

    def places(self, a, b, z_to):
        dz = lax.rem(z_to - self.z + 4, 4)
        ab = a + b
        first = jnp.where(dz == 0, 3 * ab, jnp.where(dz == 1, 2 * ab, jnp.where(dz == 2, 0, a + 2 * b)))
        second = jnp.where(
            dz == 0, 3 * ab + a, jnp.where(dz == 1, a, jnp.where(dz == 2, ab, 2 * ab + a))
        )
        return first, second

    def at(self, start, size):
        return pl.ds(pl.multiple_of(start, self.align), size)

    def start_first(self, t):
        for k in (0, 1, 2):
            self.copy(k, t).start()

    def second(self, t):
        a, b, xa, xb = self.split
        ab, xr = a + b, xa + xb
        self.copy(0, t).wait_recv()
        for i in (0, 1):
            self.zbuf[t, i, 2 * ab : 2 * ab + a] = (
                self.zbuf[t, i, 2 * ab : 2 * ab + a].astype(F32) + self.z_up1[t, i, 0:a].astype(F32)
            ).astype(self.dtype)
        self.copy(3, t).start()
        self.copy(1, t).wait_recv()
        for i in (0, 1):
            self.zbuf[t, i, 2 * ab + a : 3 * ab] = (
                self.zbuf[t, i, 2 * ab + a : 3 * ab].astype(F32) + self.z_dn1[t, i, 0:b].astype(F32)
            ).astype(self.dtype)
        self.copy(4, t).start()
        self.copy(2, t).wait_recv()
        for z_to in range(4):
            first, second = self.places(xa, xb, z_to)
            both = (
                self.cbuf[t, 0, z_to].astype(F32) + self.c_in[t, z_to].astype(F32)
            ).astype(self.dtype)
            self.xz[t, self.at(first, xa)] = both[0:xa]
            self.xz[t, self.at(second, xb)] = both[xa:xr]
        self.copy(5, t).start()
        self.copy(6, t).start()

    def third(self, t):
        a, b, xa, xb = self.split
        ab, xr = a + b, xa + xb
        self.copy(3, t).wait_recv()
        self.copy(4, t).wait_recv()
        for i in (0, 1):
            place = jnp.where(self.x == i, 0, 1)
            self.fin[t, place, 0:a] = (
                self.zbuf[t, i, 3 * ab : 3 * ab + a].astype(F32)
                + self.z_up2[t, i].astype(F32)
                + self.z_dn1[t, i, b:ab].astype(F32)
            ).astype(self.dtype)
            self.fin[t, place, a:ab] = (
                self.zbuf[t, i, 3 * ab + a : 4 * ab].astype(F32)
                + self.z_dn2[t, i].astype(F32)
                + self.z_up1[t, i, a:ab].astype(F32)
            ).astype(self.dtype)
        self.copy(7, t).start()
        self.copy(5, t).wait_recv()
        self.xz[t, 2 * xr : 2 * xr + xa] = (
            self.xz[t, 2 * xr : 2 * xr + xa].astype(F32) + self.x_up1[t, 0:xa].astype(F32)
        ).astype(self.dtype)
        self.copy(8, t).start()
        self.copy(6, t).wait_recv()
        self.xz[t, 2 * xr + xa : 3 * xr] = (
            self.xz[t, 2 * xr + xa : 3 * xr].astype(F32) + self.x_dn1[t, 0:xb].astype(F32)
        ).astype(self.dtype)
        self.copy(9, t).start()

    def last(self, t):
        a, b, xa, xb = self.split
        ab, xr = a + b, xa + xb
        self.copy(7, t).wait_recv()
        one = self.fin[t, 0].astype(F32) + self.x_last[t].astype(F32)
        self.copy(8, t).wait_recv()
        self.copy(9, t).wait_recv()
        two = (
            self.xz[t, 3 * xr : 3 * xr + xa].astype(F32)
            + self.x_up2[t].astype(F32)
            + self.x_dn1[t, xb:xr].astype(F32)
        )
        three = (
            self.xz[t, 3 * xr + xa : 4 * xr].astype(F32)
            + self.x_dn2[t].astype(F32)
            + self.x_up1[t, xa:xr].astype(F32)
        )
        return one, two, three

    def finish(self):
        for k in range(MESSAGES):
            self.copy(k, slice(0, UNITS)).wait_send()


def kernel(
    x_hbm, gain_hbm, wq_hbm, wkv_hbm, wg_hbm, wu_hbm, k_hbm, v_hbm, len_ref,
    att_ref, hid,
    xbuf, gain, wq, wkv, wg, wu, keys, values, load_sem,
    piece, pbuf, ag_send, ag_recv, ag_side,
    qtmp, gtmp, utmp,
    qout, qin, q_send, q_recv,
    att1, att1_in, att1_send, att1_recv,
    att2, att2_in, att2_send, att2_recv,
    *sum_refs,
):
    w = lax.axis_index("wide")
    n = lax.axis_index("narrow")
    y, h, c = w // 4, lax.rem(w // 2, 2), lax.rem(w, 2)
    x, z = n // 4, lax.rem(n, 4)
    slab = piece.shape[3]
    tiles = slab // LANES
    rows = xbuf.shape[0]
    width = xbuf.shape[1]

    def wide(yy, hh, cc):
        return (yy * 2 + hh) * 2 + cc

    y_up = (wide(lax.rem(y + 1, 4), h, c), n)
    y_down = (wide(lax.rem(y + 3, 4), h, c), n)
    side = (wide(y, h, 1 - c), n)
    pair = (wide(y, 1 - h, c), (1 - x) * 4 + z)
    pair_up = (wide(lax.rem(y + 1, 4), 1 - h, c), (1 - x) * 4 + z)
    pair_down = (wide(lax.rem(y + 3, 4), 1 - h, c), (1 - x) * 4 + z)
    z_up = (w, x * 4 + lax.rem(z + 1, 4))
    z_down = (w, x * 4 + lax.rem(z + 3, 4))
    across = (w, (1 - x) * 4 + z)

    part = wg.shape[1] // PARTS
    pairs = [(x_hbm, xbuf), (gain_hbm, gain), (wq_hbm, wq), (wkv_hbm, wkv), (k_hbm, keys), (v_hbm, values)]
    for i in range(PARTS):
        cols = slice(i * part, (i + 1) * part)
        pairs += [(wg_hbm.at[:, cols], wg.at[:, cols]), (wu_hbm.at[:, cols], wu.at[:, cols])]
    loads = [pltpu.make_async_copy(src, dst, load_sem.at[i]) for i, (src, dst) in enumerate(pairs)]
    for load in loads[0:4]:
        load.start()

    barrier = pltpu.get_barrier_semaphore()
    for s in range(1, 16):
        pl.semaphore_signal(barrier, inc=1, device_id=(lax.rem(w + s, 16), n), device_id_type=MESH)
    for s in range(1, 8):
        pl.semaphore_signal(barrier, inc=1, device_id=(w, lax.rem(n + s, 8)), device_id_type=MESH)
    for other in (pair, pair_up, pair_down):
        pl.semaphore_signal(barrier, inc=1, device_id=other, device_id_type=MESH)

    loads[0].wait()
    loads[1].wait()
    for load in loads[6:]:
        load.start()
    step_cols = 1024

    def add_block(i, total):
        block = xbuf[:, pl.ds(pl.multiple_of(i * step_cols, step_cols), step_cols)].astype(F32)
        for s in range(step_cols // 256):
            total = total + block[:, s * 256 : (s + 1) * 256]
        return total

    zero = jnp.zeros((rows, 256), F32)
    total = lax.fori_loop(0, width // step_cols, add_block, zero)
    average = jnp.sum(total, axis=1, keepdims=True) * (1.0 / width)

    def add_square(i, total):
        block = xbuf[:, pl.ds(pl.multiple_of(i * step_cols, step_cols), step_cols)].astype(F32)
        block = block - average
        block = block * block
        for s in range(step_cols // 256):
            total = total + block[:, s * 256 : (s + 1) * 256]
        return total

    total = lax.fori_loop(0, width // step_cols, add_square, zero)
    spread = jnp.sum(total, axis=1, keepdims=True) * (1.0 / width)
    factor = lax.rsqrt(spread + 1e-05)

    def normed(owner, i):
        start = pl.multiple_of(owner * slab + i * LANES, LANES)
        block = xbuf[:, pl.ds(start, LANES)].astype(F32)
        return ((block - average) * factor * gain[pl.ds(owner * tiles + i, 1), :]).astype(BF16)

    pair_n = (1 - x) * 4 + z
    for i in range(tiles):
        pbuf[:, i * LANES : (i + 1) * LANES] = normed(pair_n, i)
    for i in range(tiles):
        piece[0, c, :, i * LANES : (i + 1) * LANES] = normed(n, i)

    pl.semaphore_wait(barrier, 25)

    def gather_copy(k):
        src, slot, to = [
            (pbuf, 1, pair),
            (piece.at[0, c], 2, y_up),
            (piece.at[0, c], 3, y_down),
            (pbuf, 4, pair_up),
            (pbuf, 5, pair_down),
            (piece.at[2, c], 6, y_up),
            (piece.at[5, c], 7, y_down),
        ][k]
        return pltpu.make_async_remote_copy(
            src_ref=src, dst_ref=piece.at[slot, c], send_sem=ag_send.at[0], recv_sem=ag_recv.at[k],
            device_id=to, device_id_type=MESH,
        )

    def side_copy(t):
        return pltpu.make_async_remote_copy(
            src_ref=piece.at[t, c], dst_ref=piece.at[t, c], send_sem=ag_send.at[1],
            recv_sem=ag_side.at[t], device_id=side, device_id_type=MESH,
        )

    def side_wait(t):
        pltpu.make_async_remote_copy(
            src_ref=piece.at[t, 1 - c], dst_ref=piece.at[t, 1 - c], send_sem=ag_send.at[1],
            recv_sem=ag_side.at[t], device_id=side, device_id_type=MESH,
        ).wait_recv()

    side_copy(0).start()
    for k in (1, 2, 0, 3, 4):
        gather_copy(k).start()

    count = len(sum_refs) // 2
    q_sum = Summer(Q_SPLIT, F32, sum_refs[:count], (x, z), z_up, z_down, across)
    h_sum = Summer(H_SPLIT, BF16, sum_refs[count:], (x, z), z_up, z_down, across)

    def chip_of(t):
        group, odd = t // 2, lax.rem(t, 2)
        dy = jnp.where(group == 0, 0, jnp.where(group == 3, 2, jnp.where(odd == 0, 3, 1)))
        flip = jnp.where((group == 0) | (group == 3), odd, group - 1)
        return lax.rem(y + dy, 4), lax.rem(h + flip, 2)

    def project_q(t, count):
        size = count * 2 * rows
        for u in range(count):
            side_wait(t + u)
        block = piece[pl.ds(t, count)].reshape(size, slab)
        for s in range(3):
            qtmp[0:size, s * 256 : (s + 1) * 256] = jnp.dot(
                block, wq[:, s * 256 : (s + 1) * 256], preferred_element_type=F32
            )
        qtmp[0:size, 768:896] = jnp.zeros((size, LANES), F32)
        qtmp[0:size, 768:800] = lax.dot_general(
            block, wkv[...], (((1,), (1,)), ((), ())), preferred_element_type=F32
        )
        qtmp[0:size, 768:896] = pltpu.roll(qtmp[0:size, 768:896], 32 * lax.rem(w, 4), axis=1)

    def pack_q(t, base):
        low = lax.broadcasted_iota(jnp.int32, (8, 896), 0) < 4
        for m in range(4):
            top = qtmp[pl.ds(pl.multiple_of(base + 8 * m, 8), 8), :]
            bottom = qtmp[pl.ds(pl.multiple_of(base + rows + 8 * m, 8), 8), :]
            even = jnp.where(low, top, pltpu.roll(bottom, 4, axis=0))
            odd = jnp.where(low, pltpu.roll(top, 4, axis=0), bottom)
            for to, block in ((2 * m, even), (2 * m + 1, odd)):
                x_to, z_to = to // 4, to % 4
                first, second = q_sum.places(16, 16, z_to)
                far = jnp.where(x == x_to, 0, 1)
                for s in range(2):
                    q_sum.zbuf[t, x_to, q_sum.at(first + 8 * s, 8)] = block[:, s * 128 : (s + 1) * 128]
                    q_sum.zbuf[t, x_to, q_sum.at(second + 8 * s, 8)] = block[
                        :, (2 + s) * 128 : (3 + s) * 128
                    ]
                for s in range(3):
                    q_sum.cbuf[t, far, z_to, 8 * s : 8 * s + 8] = block[:, (4 + s) * 128 : (5 + s) * 128]
        q_sum.start_first(t)

    def pass_on(t):
        pltpu.make_async_remote_copy(
            src_ref=pbuf, dst_ref=piece.at[t, c], send_sem=ag_send.at[0],
            recv_sem=ag_recv.at[t - 1], device_id=side, device_id_type=MESH,
        ).wait_recv()
        side_copy(t).start()
        for slot, k in ((2, 5), (5, 6)):

            @pl.when(t == slot)
            def _():
                gather_copy(k).start()

    def project_h(t, count, first):
        size = count * 2 * rows
        block = piece[pl.ds(t, count)].reshape(size, slab)
        for s in range(gtmp.shape[1] // 256):
            if s * 256 % part == 0:

                @pl.when(first)
                def _():
                    loads[6 + 2 * (s * 256 // part)].wait()
                    loads[7 + 2 * (s * 256 // part)].wait()


            cols = slice(s * 256, (s + 1) * 256)
            gtmp[0:size, cols] = jnp.dot(block, wg[:, cols], preferred_element_type=F32).astype(BF16)
            utmp[0:size, cols] = jnp.dot(block, wu[:, cols], preferred_element_type=F32).astype(BF16)

    def pack_h(t, low):
        for to in range(8):
            x_to, z_to = to // 4, to % 4
            first, second = h_sum.places(80, 80, z_to)
            far = jnp.where(x == x_to, 0, 1)
            start = 288 * to
            base = start // LANES * LANES
            stop = min(-(-(start + 288) // LANES) * LANES, gtmp.shape[1])
            off = start - base
            g = gtmp[pl.ds(pl.multiple_of(low, 64), 2 * rows), base:stop]
            u = utmp[pl.ds(pl.multiple_of(low, 64), 2 * rows), base:stop]
            g0, g1, gr = g[:, off : off + 128], g[:, off + 128 : off + 256], g[:, off + 256 : off + 288]
            u0, u1, ur = u[:, off : off + 128], u[:, off + 128 : off + 256], u[:, off + 256 : off + 288]
            h_sum.zbuf[t, x_to, h_sum.at(first, 64)] = g0
            h_sum.zbuf[t, x_to, h_sum.at(first + 64, 16)] = g1[0:16]
            h_sum.zbuf[t, x_to, h_sum.at(second, 48)] = g1[16:64]
            h_sum.zbuf[t, x_to, h_sum.at(second + 48, 32)] = u0[0:32]
            h_sum.cbuf[t, far, z_to, 0:32] = u0[32:64]
            h_sum.cbuf[t, far, z_to, 32:96] = u1
            h_sum.cbuf[t, far, z_to, 96:128, 0:32] = gr[0:32]
            h_sum.cbuf[t, far, z_to, 96:128, 32:64] = ur[0:32]
            h_sum.cbuf[t, far, z_to, 96:128, 64:96] = gr[32:64]
            h_sum.cbuf[t, far, z_to, 96:128, 96:128] = ur[32:64]
        h_sum.start_first(t)

    def q_copy(t, core):
        yy, hh = chip_of(t)
        to = wide(yy, hh, core)
        return to, pltpu.make_async_remote_copy(
            src_ref=qout.at[t, core], dst_ref=qin.at[w], send_sem=q_send.at[0],
            recv_sem=q_recv.at[0], device_id=(to, n), device_id_type=MESH,
        )

    def finish_q(t):
        one, two, three = q_sum.last(t)
        blocks = [one[8 * s : 8 * s + 8] for s in range(4)]
        blocks += [two[0:8], two[8:16], three]
        blocks = [block.astype(BF16).astype(F32) for block in blocks]
        for core in range(2):
            for s, block in enumerate(blocks):
                qout[t, core, :, s * 128 : (s + 1) * 128] = block[4 * core : 4 * core + 4]
            to, copy = q_copy(t, core)

            @pl.when(to != w)
            def _():
                copy.start()

            @pl.when(to == w)
            def _():
                for s, block in enumerate(blocks):
                    qin[w, :, s * 128 : (s + 1) * 128] = block[4 * core : 4 * core + 4]

    def silu(v):
        return v / (1.0 + jnp.exp(-v))

    def finish_h(t):
        one, two, three = h_sum.last(t)
        yy, hh = chip_of(t)
        start = (yy * 2 + hh) * 64

        def out_rows(offset, size):
            return pl.ds(pl.multiple_of(start + offset, 32), size)

        hid[out_rows(0, 32), 0:128] = (silu(one[0:32]) * one[128:160]).astype(BF16)
        hid[out_rows(32, 32), 0:128] = (silu(one[32:64]) * two[0:32]).astype(BF16)
        hid[out_rows(0, 32), 128:256] = (silu(one[64:96]) * two[32:64]).astype(BF16)
        hid[out_rows(32, 32), 128:256] = (silu(one[96:128]) * three[0:32]).astype(BF16)
        rest = three[32:64]
        rest = silu(rest) * pltpu.roll(rest, 96, axis=1)
        hid[out_rows(0, 32), 256:288] = rest[:, 0:32].astype(BF16)
        hid[out_rows(32, 32), 256:288] = pltpu.roll(rest, 64, axis=1)[:, 0:32].astype(BF16)

    def wait_all(buffer, send, recv):
        part = buffer.at[0 : buffer.shape[0] - 1]
        return pltpu.make_async_remote_copy(
            src_ref=part, dst_ref=part, send_sem=send.at[0], recv_sem=recv.at[0],
            device_id=side, device_id_type=MESH,
        )

    def att1_copy(s):
        to = lax.rem(n + s, 8)
        return pltpu.make_async_remote_copy(
            src_ref=att1.at[to], dst_ref=att1_in.at[n], send_sem=att1_send.at[0],
            recv_sem=att1_recv.at[0], device_id=(w, to), device_id_type=MESH,
        )

    def att2_copy(s):
        to = lax.rem(w + s, 16)
        return pltpu.make_async_remote_copy(
            src_ref=att2.at[to], dst_ref=att2_in.at[w], send_sem=att2_send.at[0],
            recv_sem=att2_recv.at[0], device_id=(to, n), device_id_type=MESH,
        )

    def attend():
        loads[4].wait()
        loads[5].wait()

        wait_all(qin, q_send, q_recv).wait_recv()

        scale = 256 ** (-0.5)
        for r in range(4):
            heads = jnp.concatenate(
                [qin[:, r, s * 256 : (s + 1) * 256] for s in range(3)], axis=0
            )
            kv = qin[:, r, 768:896]
            kv = [jnp.sum(kv[4 * i : 4 * i + 4], axis=0, keepdims=True) for i in range(4)]
            own_key = jnp.concatenate(kv[0:2], axis=1)
            own_value = jnp.concatenate(kv[2:4], axis=1)
            scores = lax.dot_general(
                heads.astype(BF16), keys[r], (((1,), (1,)), ((), ())), preferred_element_type=F32
            ) * scale
            valid = lax.broadcasted_iota(jnp.int32, scores.shape, 1) < len_ref[r]
            raised = jnp.where(valid, jnp.exp(scores), 0.0)
            own = jnp.exp(jnp.sum(heads * own_key, axis=1, keepdims=True) * scale)
            total = jnp.sum(raised, axis=1, keepdims=True) + own
            probs = (raised / total).astype(BF16)
            own_prob = (own / total).astype(BF16).astype(F32)
            out = jnp.dot(probs, values[r], preferred_element_type=F32) + own_prob * own_value
            flat = jnp.concatenate(
                [out[0:16], out[16:32], out[32:48], jnp.zeros((16, LANES), F32)], axis=1
            )
            for to in range(8):
                att1[to, r] = flat[:, 96 * to : 96 * to + 128].astype(BF16)
        att1_in[n] = att1[n]
        for s in range(1, 8):
            att1_copy(s).start()

    def spread_heads():
        wait_all(att1_in, att1_send, att1_recv).wait_recv()
        att2[...] = jnp.swapaxes(att1_in[...].reshape(32, 16, LANES), 0, 1)
        att2_in[w] = att2[w]
        for s in range(1, 16):
            att2_copy(s).start()

    def gather_heads():
        wait_all(att2_in, att2_send, att2_recv).wait_recv()
        att_ref[...] = att2_in[...].reshape(512, LANES)

    def look_up(i, table):
        start, count = jnp.int32(0), jnp.int32(0)
        for at, (first, size) in table.items():
            start = jnp.where(i == at, first, start)
            count = jnp.where(i == at, size, count)
        return start, count

    def run(i, table, step):
        start, count = look_up(i, table)

        @pl.loop(0, count)
        def _(u):
            step(start + u)

    def project(i, table, step, pack, *more):
        start, count = look_up(i, table)
        for size in sorted({size for _, size in table.values()}):

            @pl.when(count == size)
            def _():
                step(start, size, *more)

        @pl.loop(0, count)
        def _(u):
            pack(start + u, u * 2 * rows)

    first_h = min(H_PROJECT)
    loads[2].wait()
    loads[3].wait()

    @pl.loop(0, PASSES)
    def _(i):
        run(i, GATHER, pass_on)
        project(i, Q_PROJECT, project_q, pack_q)
        project(i, H_PROJECT, project_h, pack_h, i == first_h)

        @pl.when(i == first_h)
        def _():
            loads[4].start()
            loads[5].start()

        run(i, Q_SECOND, q_sum.second)
        run(i, Q_THIRD, q_sum.third)
        run(i, H_SECOND, h_sum.second)
        run(i, H_THIRD, h_sum.third)
        run(i, Q_LAST, finish_q)
        run(i, H_LAST, finish_h)

        @pl.when(i == ATTEND)
        def _():
            attend()

        @pl.when(i == SPREAD)
        def _():
            spread_heads()

    gather_heads()

    for part, sem in ((piece.at[0:7, 0], 0), (piece.at[:, 0], 1)):
        pltpu.make_async_remote_copy(
            src_ref=part, dst_ref=part, send_sem=ag_send.at[sem], recv_sem=ag_recv.at[0],
            device_id=side, device_id_type=MESH,
        ).wait_send()
    q_sum.finish()
    h_sum.finish()
    wait_all(qin, q_send, q_recv).wait_send()
    wait_all(att1_in, att1_send, att1_recv).wait_send()
    wait_all(att2_in, att2_send, att2_recv).wait_send()


def turn(att, hid, att_out, hid_out):
    for i in range(4):
        cols = slice(i * 128, (i + 1) * 128)
        att_out[:, cols] = att[cols, :].T[0:96]
        hid_out[0:128, cols] = hid[cols, 0:128].T
        hid_out[128:256, cols] = hid[cols, 128:256].T
        hid_out[256:288, cols] = hid[cols, 256:384].T[0:32]


def body(
    layer_input, norm_gain, w_query, w_keyvalue, w_gate, w_up, key_cache, value_cache, cache_lengths
):
    rows, width = layer_input.shape
    slab = w_query.shape[0]
    anywhere = pl.BlockSpec(memory_space=pl.ANY)
    vmem = pl.BlockSpec(memory_space=pltpu.VMEM)
    dma = pltpu.SemaphoreType.DMA
    attended, hidden = pl.pallas_call(
        kernel,
        out_shape=(
            jax.ShapeDtypeStruct((512, LANES), BF16),
            jax.ShapeDtypeStruct((512, 3 * LANES), BF16),
        ),
        in_specs=[anywhere] * 8 + [pl.BlockSpec(memory_space=pltpu.SMEM)],
        out_specs=(vmem, vmem),
        scratch_shapes=[
            pltpu.VMEM((rows, width), BF16),
            pltpu.VMEM((width // LANES, LANES), F32),
            pltpu.VMEM(w_query.shape, BF16),
            pltpu.VMEM(w_keyvalue.shape[::-1], BF16),
            pltpu.VMEM(w_gate.shape, BF16),
            pltpu.VMEM(w_up.shape, BF16),
            pltpu.VMEM(key_cache.shape, BF16),
            pltpu.VMEM(value_cache.shape, BF16),
            dma((6 + 2 * PARTS,)),
            pltpu.VMEM((UNITS, 2, rows, slab), BF16),
            pltpu.VMEM((rows, slab), BF16),
            dma((2,)),
            dma((7,)),
            dma((8,)),
            pltpu.VMEM((4 * rows, 896), F32),
            pltpu.VMEM((4 * rows, w_gate.shape[1]), BF16),
            pltpu.VMEM((4 * rows, w_up.shape[1]), BF16),
            pltpu.VMEM((UNITS, 2, 4, 896), F32),
            pltpu.VMEM((16, 4, 896), F32),
            dma((1,)),
            dma((1,)),
            pltpu.VMEM((8, 4, 16, LANES), BF16),
            pltpu.VMEM((8, 4, 16, LANES), BF16),
            dma((1,)),
            dma((1,)),
            pltpu.VMEM((16, 32, LANES), BF16),
            pltpu.VMEM((16, 32, LANES), BF16),
            dma((1,)),
            dma((1,)),
        ]
        + sum_scratch(Q_SPLIT, F32)
        + sum_scratch(H_SPLIT, BF16),
        compiler_params=pltpu.CompilerParams(
            collective_id=0, has_side_effects=True, vmem_limit_bytes=60 * 1024 * 1024
        ),
    )(
        layer_input, norm_gain.reshape(width // LANES, LANES), w_query, w_keyvalue.T, w_gate, w_up,
        key_cache, value_cache, cache_lengths,
    )
    attended, hidden = pl.pallas_call(
        turn,
        out_shape=(
            jax.ShapeDtypeStruct((96, 512), BF16),
            jax.ShapeDtypeStruct((288, 512), BF16),
        ),
        in_specs=[vmem, vmem],
        out_specs=(vmem, vmem),
    )(attended, hidden)
    return attended.T, hidden.T


def solution(mesh):
    placed = (
        P("wide", None),
        P(),
        P("narrow", "wide"),
        P("narrow", "wide"),
        P("narrow", "wide"),
        P("narrow", "wide"),
        P(("wide", "narrow"), None, None),
        P(("wide", "narrow"), None, None),
        P(("wide", "narrow")),
    )
    return jax.shard_map(
        body,
        mesh=mesh,
        in_specs=placed,
        out_specs=(P(None, ("wide", "narrow")), P(None, ("wide", "narrow"))),
        check_vma=False,
    )
```

```python
import functools

import jax
import jax.numpy as jnp
from jax import lax
from jax.experimental import pallas as pl
from jax.experimental.pallas import tpu as pltpu
from jax.sharding import PartitionSpec as P

MESH = pl.DeviceIdType.MESH
F32 = jnp.float32
BF16 = jnp.bfloat16
UNITS = 8
LANES = 128
Q_SPLIT = (16, 16, 16, 8)
H_SPLIT = (80, 80, 64, 64)
MESSAGES = 10
PARTS = 3
GATHER = {
    1: (1, 3), 4: (5, 1), 5: (4, 1), 6: (6, 1), 7: (7, 1),
}
Q_PROJECT = {
    0: (0, 1), 2: (1, 1), 3: (2, 2), 7: (4, 2), 8: (6, 2),
}
H_PROJECT = {
    4: (0, 2), 8: (6, 2), 13: (2, 2), 18: (4, 2),
}
Q_SECOND = {
    1: (0, 1), 4: (1, 1), 6: (2, 2), 9: (4, 1), 10: (5, 2), 12: (7, 1),
}
Q_THIRD = {
    8: (0, 1), 9: (1, 1), 10: (3, 1), 11: (2, 1), 14: (4, 1), 15: (6, 1), 16: (5, 1), 17: (7, 1),
}
H_SECOND = {
    10: (0, 1), 15: (1, 1), 17: (6, 1), 19: (3, 1), 20: (2, 1), 21: (7, 1), 23: (5, 1), 25: (4, 1),
}
H_THIRD = {
    19: (0, 1), 22: (1, 1), 23: (6, 1), 24: (2, 1), 26: (5, 1), 27: (3, 1), 29: (7, 1), 30: (4, 1),
}
Q_LAST = {
    13: (0, 1), 18: (1, 3), 20: (4, 1), 21: (5, 3),
}
H_LAST = {
    27: (6, 1), 28: (1, 2), 31: (5, 1), 32: (7, 1), 33: (4, 1), 34: (0, 1), 35: (3, 1),
}
ATTEND = 25
SPREAD = 30
PASSES = 36


def sum_scratch(split, dtype):
    a, b, xa, xb = split
    ab, xr = a + b, xa + xb
    n = UNITS
    return [
        pltpu.VMEM((n, 2, 4 * ab, LANES), dtype),
        pltpu.VMEM((n, 2, ab, LANES), dtype),
        pltpu.VMEM((n, 2, ab, LANES), dtype),
        pltpu.VMEM((n, 2, a, LANES), dtype),
        pltpu.VMEM((n, 2, b, LANES), dtype),
        pltpu.VMEM((n, 2, ab, LANES), dtype),
        pltpu.VMEM((n, ab, LANES), dtype),
        pltpu.VMEM((n, 2, 4, xr, LANES), dtype),
        pltpu.VMEM((n, 4, xr, LANES), dtype),
        pltpu.VMEM((n, 4 * xr, LANES), dtype),
        pltpu.VMEM((n, xr, LANES), dtype),
        pltpu.VMEM((n, xr, LANES), dtype),
        pltpu.VMEM((n, xa, LANES), dtype),
        pltpu.VMEM((n, xb, LANES), dtype),
        pltpu.SemaphoreType.DMA((MESSAGES,)),
        pltpu.SemaphoreType.DMA((n, MESSAGES)),
    ]


class Summer:
    def __init__(self, split, dtype, refs, here, up, down, across):
        self.split, self.dtype = split, dtype
        (
            self.zbuf, self.z_up1, self.z_dn1, self.z_up2, self.z_dn2, self.fin, self.x_last,
            self.cbuf, self.c_in, self.xz, self.x_up1, self.x_dn1, self.x_up2, self.x_dn2,
            self.send, self.recv,
        ) = refs
        self.x, self.z = here
        self.up, self.down, self.across = up, down, across
        self.align = 16 if dtype == BF16 else 8

    def copy(self, k, t):
        a, b, xa, xb = self.split
        ab, xr = a + b, xa + xb
        src, dst, to = [
            (self.zbuf.at[t, :, 0:ab], self.z_up1.at[t], self.up),
            (self.zbuf.at[t, :, ab : 2 * ab], self.z_dn1.at[t], self.down),
            (self.cbuf.at[t, 1], self.c_in.at[t], self.across),
            (self.zbuf.at[t, :, 2 * ab : 2 * ab + a], self.z_up2.at[t], self.up),
            (self.zbuf.at[t, :, 2 * ab + a : 3 * ab], self.z_dn2.at[t], self.down),
            (self.xz.at[t, 0:xr], self.x_up1.at[t], self.up),
            (self.xz.at[t, xr : 2 * xr], self.x_dn1.at[t], self.down),
            (self.fin.at[t, 1], self.x_last.at[t], self.across),
            (self.xz.at[t, 2 * xr : 2 * xr + xa], self.x_up2.at[t], self.up),
            (self.xz.at[t, 2 * xr + xa : 3 * xr], self.x_dn2.at[t], self.down),
        ][k]
        return pltpu.make_async_remote_copy(
            src_ref=src, dst_ref=dst, send_sem=self.send.at[k], recv_sem=self.recv.at[0 if isinstance(t, slice) else t, k],
            device_id=to, device_id_type=MESH,
        )

    def places(self, a, b, z_to):
        dz = lax.rem(z_to - self.z + 4, 4)
        ab = a + b
        first = jnp.where(dz == 0, 3 * ab, jnp.where(dz == 1, 2 * ab, jnp.where(dz == 2, 0, a + 2 * b)))
        second = jnp.where(
            dz == 0, 3 * ab + a, jnp.where(dz == 1, a, jnp.where(dz == 2, ab, 2 * ab + a))
        )
        return first, second

    def at(self, start, size):
        return pl.ds(pl.multiple_of(start, self.align), size)

    def start_first(self, t):
        for k in (0, 1, 2):
            self.copy(k, t).start()

    def second(self, t):
        a, b, xa, xb = self.split
        ab, xr = a + b, xa + xb
        self.copy(0, t).wait_recv()
        for i in (0, 1):
            self.zbuf[t, i, 2 * ab : 2 * ab + a] = (
                self.zbuf[t, i, 2 * ab : 2 * ab + a].astype(F32) + self.z_up1[t, i, 0:a].astype(F32)
            ).astype(self.dtype)
        self.copy(3, t).start()
        self.copy(1, t).wait_recv()
        for i in (0, 1):
            self.zbuf[t, i, 2 * ab + a : 3 * ab] = (
                self.zbuf[t, i, 2 * ab + a : 3 * ab].astype(F32) + self.z_dn1[t, i, 0:b].astype(F32)
            ).astype(self.dtype)
        self.copy(4, t).start()
        self.copy(2, t).wait_recv()
        for z_to in range(4):
            first, second = self.places(xa, xb, z_to)
            both = (
                self.cbuf[t, 0, z_to].astype(F32) + self.c_in[t, z_to].astype(F32)
            ).astype(self.dtype)
            self.xz[t, self.at(first, xa)] = both[0:xa]
            self.xz[t, self.at(second, xb)] = both[xa:xr]
        self.copy(5, t).start()
        self.copy(6, t).start()

    def third(self, t):
        a, b, xa, xb = self.split
        ab, xr = a + b, xa + xb
        self.copy(3, t).wait_recv()
        self.copy(4, t).wait_recv()
        for i in (0, 1):
            place = jnp.where(self.x == i, 0, 1)
            self.fin[t, place, 0:a] = (
                self.zbuf[t, i, 3 * ab : 3 * ab + a].astype(F32)
                + self.z_up2[t, i].astype(F32)
                + self.z_dn1[t, i, b:ab].astype(F32)
            ).astype(self.dtype)
            self.fin[t, place, a:ab] = (
                self.zbuf[t, i, 3 * ab + a : 4 * ab].astype(F32)
                + self.z_dn2[t, i].astype(F32)
                + self.z_up1[t, i, a:ab].astype(F32)
            ).astype(self.dtype)
        self.copy(7, t).start()
        self.copy(5, t).wait_recv()
        self.xz[t, 2 * xr : 2 * xr + xa] = (
            self.xz[t, 2 * xr : 2 * xr + xa].astype(F32) + self.x_up1[t, 0:xa].astype(F32)
        ).astype(self.dtype)
        self.copy(8, t).start()
        self.copy(6, t).wait_recv()
        self.xz[t, 2 * xr + xa : 3 * xr] = (
            self.xz[t, 2 * xr + xa : 3 * xr].astype(F32) + self.x_dn1[t, 0:xb].astype(F32)
        ).astype(self.dtype)
        self.copy(9, t).start()

    def last(self, t):
        a, b, xa, xb = self.split
        ab, xr = a + b, xa + xb
        self.copy(7, t).wait_recv()
        one = self.fin[t, 0].astype(F32) + self.x_last[t].astype(F32)
        self.copy(8, t).wait_recv()
        self.copy(9, t).wait_recv()
        two = (
            self.xz[t, 3 * xr : 3 * xr + xa].astype(F32)
            + self.x_up2[t].astype(F32)
            + self.x_dn1[t, xb:xr].astype(F32)
        )
        three = (
            self.xz[t, 3 * xr + xa : 4 * xr].astype(F32)
            + self.x_dn2[t].astype(F32)
            + self.x_up1[t, xa:xr].astype(F32)
        )
        return one, two, three

    def finish(self):
        for k in range(MESSAGES):
            self.copy(k, slice(0, UNITS)).wait_send()


def kernel(
    x_hbm, gain_hbm, wq_hbm, wkv_hbm, wg_hbm, wu_hbm, k_hbm, v_hbm, len_ref,
    att_ref, hid,
    xbuf, gain, wq, wkv, wg, wu, keys, values, load_sem,
    piece, pbuf, ag_send, ag_recv, ag_side,
    qtmp, gtmp, utmp,
    qout, qin, q_send, q_recv,
    att1, att1_in, att1_send, att1_recv,
    att2, att2_in, att2_send, att2_recv,
    *sum_refs,
):
    w = lax.axis_index("wide")
    n = lax.axis_index("narrow")
    y, h, c = w // 4, lax.rem(w // 2, 2), lax.rem(w, 2)
    x, z = n // 4, lax.rem(n, 4)
    slab = piece.shape[3]
    tiles = slab // LANES
    rows = xbuf.shape[0]
    width = xbuf.shape[1]

    def wide(yy, hh, cc):
        return (yy * 2 + hh) * 2 + cc

    y_up = (wide(lax.rem(y + 1, 4), h, c), n)
    y_down = (wide(lax.rem(y + 3, 4), h, c), n)
    side = (wide(y, h, 1 - c), n)
    pair = (wide(y, 1 - h, c), (1 - x) * 4 + z)
    pair_up = (wide(lax.rem(y + 1, 4), 1 - h, c), (1 - x) * 4 + z)
    pair_down = (wide(lax.rem(y + 3, 4), 1 - h, c), (1 - x) * 4 + z)
    z_up = (w, x * 4 + lax.rem(z + 1, 4))
    z_down = (w, x * 4 + lax.rem(z + 3, 4))
    across = (w, (1 - x) * 4 + z)

    part = wg.shape[1] // PARTS
    pairs = [(x_hbm, xbuf), (gain_hbm, gain), (wq_hbm, wq), (wkv_hbm, wkv), (k_hbm, keys), (v_hbm, values)]
    for i in range(PARTS):
        cols = slice(i * part, (i + 1) * part)
        pairs += [(wg_hbm.at[:, cols], wg.at[:, cols]), (wu_hbm.at[:, cols], wu.at[:, cols])]
    loads = [pltpu.make_async_copy(src, dst, load_sem.at[i]) for i, (src, dst) in enumerate(pairs)]
    for load in loads[0:4]:
        load.start()

    barrier = pltpu.get_barrier_semaphore()
    for s in range(1, 16):
        pl.semaphore_signal(barrier, inc=1, device_id=(lax.rem(w + s, 16), n), device_id_type=MESH)
    for s in range(1, 8):
        pl.semaphore_signal(barrier, inc=1, device_id=(w, lax.rem(n + s, 8)), device_id_type=MESH)
    for other in (pair, pair_up, pair_down):
        pl.semaphore_signal(barrier, inc=1, device_id=other, device_id_type=MESH)

    loads[0].wait()
    loads[1].wait()
    for load in loads[6:]:
        load.start()
    step_cols = 1024

    def add_block(i, total):
        block = xbuf[:, pl.ds(pl.multiple_of(i * step_cols, step_cols), step_cols)].astype(F32)
        for s in range(step_cols // 256):
            total = total + block[:, s * 256 : (s + 1) * 256]
        return total

    zero = jnp.zeros((rows, 256), F32)
    total = lax.fori_loop(0, width // step_cols, add_block, zero)
    average = jnp.sum(total, axis=1, keepdims=True) * (1.0 / width)

    def add_square(i, total):
        block = xbuf[:, pl.ds(pl.multiple_of(i * step_cols, step_cols), step_cols)].astype(F32)
        block = block - average
        block = block * block
        for s in range(step_cols // 256):
            total = total + block[:, s * 256 : (s + 1) * 256]
        return total

    total = lax.fori_loop(0, width // step_cols, add_square, zero)
    spread = jnp.sum(total, axis=1, keepdims=True) * (1.0 / width)
    factor = lax.rsqrt(spread + 1e-05)

    def normed(owner, i):
        start = pl.multiple_of(owner * slab + i * LANES, LANES)
        block = xbuf[:, pl.ds(start, LANES)].astype(F32)
        return ((block - average) * factor * gain[pl.ds(owner * tiles + i, 1), :]).astype(BF16)

    pair_n = (1 - x) * 4 + z
    for i in range(tiles):
        pbuf[:, i * LANES : (i + 1) * LANES] = normed(pair_n, i)
    for i in range(tiles):
        piece[0, c, :, i * LANES : (i + 1) * LANES] = normed(n, i)

    pl.semaphore_wait(barrier, 25)

    def gather_copy(k):
        src, slot, to = [
            (pbuf, 1, pair),
            (piece.at[0, c], 2, y_up),
            (piece.at[0, c], 3, y_down),
            (pbuf, 4, pair_up),
            (pbuf, 5, pair_down),
            (piece.at[2, c], 6, y_up),
            (piece.at[5, c], 7, y_down),
        ][k]
        return pltpu.make_async_remote_copy(
            src_ref=src, dst_ref=piece.at[slot, c], send_sem=ag_send.at[0], recv_sem=ag_recv.at[k],
            device_id=to, device_id_type=MESH,
        )

    def side_copy(t):
        return pltpu.make_async_remote_copy(
            src_ref=piece.at[t, c], dst_ref=piece.at[t, c], send_sem=ag_send.at[1],
            recv_sem=ag_side.at[t], device_id=side, device_id_type=MESH,
        )

    def side_wait(t):
        pltpu.make_async_remote_copy(
            src_ref=piece.at[t, 1 - c], dst_ref=piece.at[t, 1 - c], send_sem=ag_send.at[1],
            recv_sem=ag_side.at[t], device_id=side, device_id_type=MESH,
        ).wait_recv()

    side_copy(0).start()
    for k in (1, 2, 0, 3, 4):
        gather_copy(k).start()

    count = len(sum_refs) // 2
    q_sum = Summer(Q_SPLIT, F32, sum_refs[:count], (x, z), z_up, z_down, across)
    h_sum = Summer(H_SPLIT, BF16, sum_refs[count:], (x, z), z_up, z_down, across)

    def chip_of(t):
        group, odd = t // 2, lax.rem(t, 2)
        dy = jnp.where(group == 0, 0, jnp.where(group == 3, 2, jnp.where(odd == 0, 3, 1)))
        flip = jnp.where((group == 0) | (group == 3), odd, group - 1)
        return lax.rem(y + dy, 4), lax.rem(h + flip, 2)

    def project_q(t, count):
        size = count * 2 * rows
        for u in range(count):
            side_wait(t + u)
        block = piece[pl.ds(t, count)].reshape(size, slab)
        for s in range(3):
            qtmp[0:size, s * 256 : (s + 1) * 256] = jnp.dot(
                block, wq[:, s * 256 : (s + 1) * 256], preferred_element_type=F32
            )
        qtmp[0:size, 768:896] = jnp.zeros((size, LANES), F32)
        qtmp[0:size, 768:800] = lax.dot_general(
            block, wkv[...], (((1,), (1,)), ((), ())), preferred_element_type=F32
        )
        qtmp[0:size, 768:896] = pltpu.roll(qtmp[0:size, 768:896], 32 * lax.rem(w, 4), axis=1)

    def pack_q(t, base):
        low = lax.broadcasted_iota(jnp.int32, (8, 896), 0) < 4
        for m in range(4):
            top = qtmp[pl.ds(pl.multiple_of(base + 8 * m, 8), 8), :]
            bottom = qtmp[pl.ds(pl.multiple_of(base + rows + 8 * m, 8), 8), :]
            even = jnp.where(low, top, pltpu.roll(bottom, 4, axis=0))
            odd = jnp.where(low, pltpu.roll(top, 4, axis=0), bottom)
            for to, block in ((2 * m, even), (2 * m + 1, odd)):
                x_to, z_to = to // 4, to % 4
                first, second = q_sum.places(16, 16, z_to)
                far = jnp.where(x == x_to, 0, 1)
                for s in range(2):
                    q_sum.zbuf[t, x_to, q_sum.at(first + 8 * s, 8)] = block[:, s * 128 : (s + 1) * 128]
                    q_sum.zbuf[t, x_to, q_sum.at(second + 8 * s, 8)] = block[
                        :, (2 + s) * 128 : (3 + s) * 128
                    ]
                for s in range(3):
                    q_sum.cbuf[t, far, z_to, 8 * s : 8 * s + 8] = block[:, (4 + s) * 128 : (5 + s) * 128]
        q_sum.start_first(t)

    def pass_on(t):
        pltpu.make_async_remote_copy(
            src_ref=pbuf, dst_ref=piece.at[t, c], send_sem=ag_send.at[0],
            recv_sem=ag_recv.at[t - 1], device_id=side, device_id_type=MESH,
        ).wait_recv()
        side_copy(t).start()
        for slot, k in ((2, 5), (5, 6)):

            @pl.when(t == slot)
            def _():
                gather_copy(k).start()

    def project_h(t, count, first):
        size = count * 2 * rows
        block = piece[pl.ds(t, count)].reshape(size, slab)
        for s in range(gtmp.shape[1] // 256):
            if s * 256 % part == 0:

                @pl.when(first)
                def _():
                    loads[6 + 2 * (s * 256 // part)].wait()
                    loads[7 + 2 * (s * 256 // part)].wait()


            cols = slice(s * 256, (s + 1) * 256)
            gtmp[0:size, cols] = jnp.dot(block, wg[:, cols], preferred_element_type=F32).astype(BF16)
            utmp[0:size, cols] = jnp.dot(block, wu[:, cols], preferred_element_type=F32).astype(BF16)

    def pack_h(t, low):
        for to in range(8):
            x_to, z_to = to // 4, to % 4
            first, second = h_sum.places(80, 80, z_to)
            far = jnp.where(x == x_to, 0, 1)
            start = 288 * to
            base = start // LANES * LANES
            stop = min(-(-(start + 288) // LANES) * LANES, gtmp.shape[1])
            off = start - base
            g = gtmp[pl.ds(pl.multiple_of(low, 64), 2 * rows), base:stop]
            u = utmp[pl.ds(pl.multiple_of(low, 64), 2 * rows), base:stop]
            g0, g1, gr = g[:, off : off + 128], g[:, off + 128 : off + 256], g[:, off + 256 : off + 288]
            u0, u1, ur = u[:, off : off + 128], u[:, off + 128 : off + 256], u[:, off + 256 : off + 288]
            h_sum.zbuf[t, x_to, h_sum.at(first, 64)] = g0
            h_sum.zbuf[t, x_to, h_sum.at(first + 64, 16)] = g1[0:16]
            h_sum.zbuf[t, x_to, h_sum.at(second, 48)] = g1[16:64]
            h_sum.zbuf[t, x_to, h_sum.at(second + 48, 32)] = u0[0:32]
            h_sum.cbuf[t, far, z_to, 0:32] = u0[32:64]
            h_sum.cbuf[t, far, z_to, 32:96] = u1
            h_sum.cbuf[t, far, z_to, 96:128, 0:32] = gr[0:32]
            h_sum.cbuf[t, far, z_to, 96:128, 32:64] = ur[0:32]
            h_sum.cbuf[t, far, z_to, 96:128, 64:96] = gr[32:64]
            h_sum.cbuf[t, far, z_to, 96:128, 96:128] = ur[32:64]
        h_sum.start_first(t)

    def q_copy(t, core):
        yy, hh = chip_of(t)
        to = wide(yy, hh, core)
        return to, pltpu.make_async_remote_copy(
            src_ref=qout.at[t, core], dst_ref=qin.at[w], send_sem=q_send.at[0],
            recv_sem=q_recv.at[0], device_id=(to, n), device_id_type=MESH,
        )

    def finish_q(t):
        one, two, three = q_sum.last(t)
        blocks = [one[8 * s : 8 * s + 8] for s in range(4)]
        blocks += [two[0:8], two[8:16], three]
        blocks = [block.astype(BF16).astype(F32) for block in blocks]
        for core in range(2):
            for s, block in enumerate(blocks):
                qout[t, core, :, s * 128 : (s + 1) * 128] = block[4 * core : 4 * core + 4]
            to, copy = q_copy(t, core)

            @pl.when(to != w)
            def _():
                copy.start()

            @pl.when(to == w)
            def _():
                for s, block in enumerate(blocks):
                    qin[w, :, s * 128 : (s + 1) * 128] = block[4 * core : 4 * core + 4]

    def silu(v):
        return v / (1.0 + jnp.exp(-v))

    def finish_h(t):
        one, two, three = h_sum.last(t)
        yy, hh = chip_of(t)
        start = (yy * 2 + hh) * 64

        def out_rows(offset, size):
            return pl.ds(pl.multiple_of(start + offset, 32), size)

        hid[out_rows(0, 32), 0:128] = (silu(one[0:32]) * one[128:160]).astype(BF16)
        hid[out_rows(32, 32), 0:128] = (silu(one[32:64]) * two[0:32]).astype(BF16)
        hid[out_rows(0, 32), 128:256] = (silu(one[64:96]) * two[32:64]).astype(BF16)
        hid[out_rows(32, 32), 128:256] = (silu(one[96:128]) * three[0:32]).astype(BF16)
        rest = three[32:64]
        rest = silu(rest) * pltpu.roll(rest, 96, axis=1)
        hid[out_rows(0, 32), 256:288] = rest[:, 0:32].astype(BF16)
        hid[out_rows(32, 32), 256:288] = pltpu.roll(rest, 64, axis=1)[:, 0:32].astype(BF16)

    def wait_all(buffer, send, recv):
        part = buffer.at[0 : buffer.shape[0] - 1]
        return pltpu.make_async_remote_copy(
            src_ref=part, dst_ref=part, send_sem=send.at[0], recv_sem=recv.at[0],
            device_id=side, device_id_type=MESH,
        )

    def att1_copy(s):
        to = lax.rem(n + s, 8)
        return pltpu.make_async_remote_copy(
            src_ref=att1.at[to], dst_ref=att1_in.at[n], send_sem=att1_send.at[0],
            recv_sem=att1_recv.at[0], device_id=(w, to), device_id_type=MESH,
        )

    def att2_copy(s):
        to = lax.rem(w + s, 16)
        return pltpu.make_async_remote_copy(
            src_ref=att2.at[to], dst_ref=att2_in.at[w], send_sem=att2_send.at[0],
            recv_sem=att2_recv.at[0], device_id=(to, n), device_id_type=MESH,
        )

    def attend():
        loads[4].wait()
        loads[5].wait()

        wait_all(qin, q_send, q_recv).wait_recv()

        scale = 256 ** (-0.5)
        for r in range(4):
            heads = jnp.concatenate(
                [qin[:, r, s * 256 : (s + 1) * 256] for s in range(3)], axis=0
            )
            kv = qin[:, r, 768:896]
            kv = [jnp.sum(kv[4 * i : 4 * i + 4], axis=0, keepdims=True) for i in range(4)]
            own_key = jnp.concatenate(kv[0:2], axis=1)
            own_value = jnp.concatenate(kv[2:4], axis=1)
            scores = lax.dot_general(
                heads.astype(BF16), keys[r], (((1,), (1,)), ((), ())), preferred_element_type=F32
            ) * scale
            valid = lax.broadcasted_iota(jnp.int32, scores.shape, 1) < len_ref[r]
            raised = jnp.where(valid, jnp.exp(scores), 0.0)
            own = jnp.exp(jnp.sum(heads * own_key, axis=1, keepdims=True) * scale)
            total = jnp.sum(raised, axis=1, keepdims=True) + own
            probs = (raised / total).astype(BF16)
            own_prob = (own / total).astype(BF16).astype(F32)
            out = jnp.dot(probs, values[r], preferred_element_type=F32) + own_prob * own_value
            flat = jnp.concatenate(
                [out[0:16], out[16:32], out[32:48], jnp.zeros((16, LANES), F32)], axis=1
            )
            for to in range(8):
                att1[to, r] = flat[:, 96 * to : 96 * to + 128].astype(BF16)
        att1_in[n] = att1[n]
        for s in range(1, 8):
            att1_copy(s).start()

    def spread_heads():
        wait_all(att1_in, att1_send, att1_recv).wait_recv()
        att2[...] = jnp.swapaxes(att1_in[...].reshape(32, 16, LANES), 0, 1)
        att2_in[w] = att2[w]
        for s in range(1, 16):
            att2_copy(s).start()

    def gather_heads():
        wait_all(att2_in, att2_send, att2_recv).wait_recv()
        att_ref[...] = att2_in[...].reshape(512, LANES)

    def look_up(i, table):
        start, count = jnp.int32(0), jnp.int32(0)
        for at, (first, size) in table.items():
            start = jnp.where(i == at, first, start)
            count = jnp.where(i == at, size, count)
        return start, count

    def run(i, table, step):
        start, count = look_up(i, table)

        @pl.loop(0, count)
        def _(u):
            step(start + u)

    def project(i, table, step, pack, *more):
        start, count = look_up(i, table)
        for size in sorted({size for _, size in table.values()}):

            @pl.when(count == size)
            def _():
                step(start, size, *more)

        @pl.loop(0, count)
        def _(u):
            pack(start + u, u * 2 * rows)

    first_h = min(H_PROJECT)
    loads[2].wait()
    loads[3].wait()

    @pl.loop(0, PASSES)
    def _(i):
        run(i, GATHER, pass_on)
        project(i, Q_PROJECT, project_q, pack_q)
        project(i, H_PROJECT, project_h, pack_h, i == first_h)

        @pl.when(i == first_h)
        def _():
            loads[4].start()
            loads[5].start()

        run(i, Q_SECOND, q_sum.second)
        run(i, Q_THIRD, q_sum.third)
        run(i, H_SECOND, h_sum.second)
        run(i, H_THIRD, h_sum.third)
        run(i, Q_LAST, finish_q)
        run(i, H_LAST, finish_h)

        @pl.when(i == ATTEND)
        def _():
            attend()

        @pl.when(i == SPREAD)
        def _():
            spread_heads()

    gather_heads()

    for part, sem in ((piece.at[0:7, 0], 0), (piece.at[:, 0], 1)):
        pltpu.make_async_remote_copy(
            src_ref=part, dst_ref=part, send_sem=ag_send.at[sem], recv_sem=ag_recv.at[0],
            device_id=side, device_id_type=MESH,
        ).wait_send()
    q_sum.finish()
    h_sum.finish()
    wait_all(qin, q_send, q_recv).wait_send()
    wait_all(att1_in, att1_send, att1_recv).wait_send()
    wait_all(att2_in, att2_send, att2_recv).wait_send()


def turn(att, hid, att_out, hid_out):
    for i in range(4):
        cols = slice(i * 128, (i + 1) * 128)
        att_out[:, cols] = att[cols, :].T[0:96]
        hid_out[0:128, cols] = hid[cols, 0:128].T
        hid_out[128:256, cols] = hid[cols, 128:256].T
        hid_out[256:288, cols] = hid[cols, 256:384].T[0:32]


def body(
    layer_input, norm_gain, w_query, w_keyvalue, w_gate, w_up, key_cache, value_cache, cache_lengths
):
    rows, width = layer_input.shape
    slab = w_query.shape[0]
    anywhere = pl.BlockSpec(memory_space=pl.ANY)
    vmem = pl.BlockSpec(memory_space=pltpu.VMEM)
    dma = pltpu.SemaphoreType.DMA
    attended, hidden = pl.pallas_call(
        kernel,
        out_shape=(
            jax.ShapeDtypeStruct((512, LANES), BF16),
            jax.ShapeDtypeStruct((512, 3 * LANES), BF16),
        ),
        in_specs=[anywhere] * 8 + [pl.BlockSpec(memory_space=pltpu.SMEM)],
        out_specs=(vmem, vmem),
        scratch_shapes=[
            pltpu.VMEM((rows, width), BF16),
            pltpu.VMEM((width // LANES, LANES), F32),
            pltpu.VMEM(w_query.shape, BF16),
            pltpu.VMEM(w_keyvalue.shape[::-1], BF16),
            pltpu.VMEM(w_gate.shape, BF16),
            pltpu.VMEM(w_up.shape, BF16),
            pltpu.VMEM(key_cache.shape, BF16),
            pltpu.VMEM(value_cache.shape, BF16),
            dma((6 + 2 * PARTS,)),
            pltpu.VMEM((UNITS, 2, rows, slab), BF16),
            pltpu.VMEM((rows, slab), BF16),
            dma((2,)),
            dma((7,)),
            dma((8,)),
            pltpu.VMEM((4 * rows, 896), F32),
            pltpu.VMEM((4 * rows, w_gate.shape[1]), BF16),
            pltpu.VMEM((4 * rows, w_up.shape[1]), BF16),
            pltpu.VMEM((UNITS, 2, 4, 896), F32),
            pltpu.VMEM((16, 4, 896), F32),
            dma((1,)),
            dma((1,)),
            pltpu.VMEM((8, 4, 16, LANES), BF16),
            pltpu.VMEM((8, 4, 16, LANES), BF16),
            dma((1,)),
            dma((1,)),
            pltpu.VMEM((16, 32, LANES), BF16),
            pltpu.VMEM((16, 32, LANES), BF16),
            dma((1,)),
            dma((1,)),
        ]
        + sum_scratch(Q_SPLIT, F32)
        + sum_scratch(H_SPLIT, BF16),
        compiler_params=pltpu.CompilerParams(
            collective_id=0, has_side_effects=True, vmem_limit_bytes=60 * 1024 * 1024
        ),
    )(
        layer_input, norm_gain.reshape(width // LANES, LANES), w_query, w_keyvalue.T, w_gate, w_up,
        key_cache, value_cache, cache_lengths,
    )
    attended, hidden = pl.pallas_call(
        turn,
        out_shape=(
            jax.ShapeDtypeStruct((96, 512), BF16),
            jax.ShapeDtypeStruct((288, 512), BF16),
        ),
        in_specs=[vmem, vmem],
        out_specs=(vmem, vmem),
    )(attended, hidden)
    return attended.T, hidden.T


def solution(mesh):
    placed = (
        P("wide", None),
        P(),
        P("narrow", "wide"),
        P("narrow", "wide"),
        P("narrow", "wide"),
        P("narrow", "wide"),
        P(("wide", "narrow"), None, None),
        P(("wide", "narrow"), None, None),
        P(("wide", "narrow")),
    )
    return jax.shard_map(
        body,
        mesh=mesh,
        in_specs=placed,
        out_specs=(P(None, ("wide", "narrow")), P(None, ("wide", "narrow"))),
        check_vma=False,
    )
```

```python
import functools

import jax
import jax.numpy as jnp
from jax import lax
from jax.experimental import pallas as pl
from jax.experimental.pallas import tpu as pltpu
from jax.sharding import PartitionSpec as P

MESH = pl.DeviceIdType.MESH
F32 = jnp.float32
BF16 = jnp.bfloat16
UNITS = 8
LANES = 128
Q_SPLIT = (16, 16, 16, 8)
H_SPLIT = (80, 80, 64, 64)
MESSAGES = 10
PARTS = 3
GATHER = {
    1: (1, 3), 4: (5, 1), 5: (4, 1), 6: (6, 1), 7: (7, 1),
}
Q_PROJECT = {
    0: (0, 1), 2: (1, 1), 3: (2, 2), 7: (4, 2), 8: (6, 2),
}
H_PROJECT = {
    4: (0, 2), 8: (6, 2), 13: (2, 2), 18: (4, 2),
}
Q_SECOND = {
    1: (0, 1), 4: (1, 1), 6: (2, 2), 9: (4, 1), 10: (5, 2), 12: (7, 1),
}
Q_THIRD = {
    8: (0, 1), 9: (1, 1), 10: (3, 1), 11: (2, 1), 14: (4, 1), 15: (6, 1), 16: (5, 1), 17: (7, 1),
}
H_SECOND = {
    10: (0, 1), 15: (1, 1), 17: (6, 1), 19: (3, 1), 20: (2, 1), 21: (7, 1), 23: (5, 1), 25: (4, 1),
}
H_THIRD = {
    19: (0, 1), 22: (1, 1), 23: (6, 1), 24: (2, 1), 26: (5, 1), 27: (3, 1), 29: (7, 1), 30: (4, 1),
}
Q_LAST = {
    13: (0, 1), 18: (1, 3), 20: (4, 1), 21: (5, 3),
}
H_LAST = {
    27: (6, 1), 28: (1, 2), 31: (5, 1), 32: (7, 1), 33: (4, 1), 34: (0, 1), 35: (3, 1),
}
ATTEND = 25
SPREAD = 30
PASSES = 36


def sum_scratch(split, dtype):
    a, b, xa, xb = split
    ab, xr = a + b, xa + xb
    n = UNITS
    return [
        pltpu.VMEM((n, 2, 4 * ab, LANES), dtype),
        pltpu.VMEM((n, 2, ab, LANES), dtype),
        pltpu.VMEM((n, 2, ab, LANES), dtype),
        pltpu.VMEM((n, 2, a, LANES), dtype),
        pltpu.VMEM((n, 2, b, LANES), dtype),
        pltpu.VMEM((n, 2, ab, LANES), dtype),
        pltpu.VMEM((n, ab, LANES), dtype),
        pltpu.VMEM((n, 2, 4, xr, LANES), dtype),
        pltpu.VMEM((n, 4, xr, LANES), dtype),
        pltpu.VMEM((n, 4 * xr, LANES), dtype),
        pltpu.VMEM((n, xr, LANES), dtype),
        pltpu.VMEM((n, xr, LANES), dtype),
        pltpu.VMEM((n, xa, LANES), dtype),
        pltpu.VMEM((n, xb, LANES), dtype),
        pltpu.SemaphoreType.DMA((MESSAGES,)),
        pltpu.SemaphoreType.DMA((n, MESSAGES)),
    ]


class Summer:
    def __init__(self, split, dtype, refs, here, up, down, across):
        self.split, self.dtype = split, dtype
        (
            self.zbuf, self.z_up1, self.z_dn1, self.z_up2, self.z_dn2, self.fin, self.x_last,
            self.cbuf, self.c_in, self.xz, self.x_up1, self.x_dn1, self.x_up2, self.x_dn2,
            self.send, self.recv,
        ) = refs
        self.x, self.z = here
        self.up, self.down, self.across = up, down, across
        self.align = 16 if dtype == BF16 else 8

    def copy(self, k, t):
        a, b, xa, xb = self.split
        ab, xr = a + b, xa + xb
        src, dst, to = [
            (self.zbuf.at[t, :, 0:ab], self.z_up1.at[t], self.up),
            (self.zbuf.at[t, :, ab : 2 * ab], self.z_dn1.at[t], self.down),
            (self.cbuf.at[t, 1], self.c_in.at[t], self.across),
            (self.zbuf.at[t, :, 2 * ab : 2 * ab + a], self.z_up2.at[t], self.up),
            (self.zbuf.at[t, :, 2 * ab + a : 3 * ab], self.z_dn2.at[t], self.down),
            (self.xz.at[t, 0:xr], self.x_up1.at[t], self.up),
            (self.xz.at[t, xr : 2 * xr], self.x_dn1.at[t], self.down),
            (self.fin.at[t, 1], self.x_last.at[t], self.across),
            (self.xz.at[t, 2 * xr : 2 * xr + xa], self.x_up2.at[t], self.up),
            (self.xz.at[t, 2 * xr + xa : 3 * xr], self.x_dn2.at[t], self.down),
        ][k]
        return pltpu.make_async_remote_copy(
            src_ref=src, dst_ref=dst, send_sem=self.send.at[k], recv_sem=self.recv.at[0 if isinstance(t, slice) else t, k],
            device_id=to, device_id_type=MESH,
        )

    def places(self, a, b, z_to):
        dz = lax.rem(z_to - self.z + 4, 4)
        ab = a + b
        first = jnp.where(dz == 0, 3 * ab, jnp.where(dz == 1, 2 * ab, jnp.where(dz == 2, 0, a + 2 * b)))
        second = jnp.where(
            dz == 0, 3 * ab + a, jnp.where(dz == 1, a, jnp.where(dz == 2, ab, 2 * ab + a))
        )
        return first, second

    def at(self, start, size):
        return pl.ds(pl.multiple_of(start, self.align), size)

    def start_first(self, t):
        for k in (0, 1, 2):
            self.copy(k, t).start()

    def second(self, t):
        a, b, xa, xb = self.split
        ab, xr = a + b, xa + xb
        self.copy(0, t).wait_recv()
        for i in (0, 1):
            self.zbuf[t, i, 2 * ab : 2 * ab + a] = (
                self.zbuf[t, i, 2 * ab : 2 * ab + a].astype(F32) + self.z_up1[t, i, 0:a].astype(F32)
            ).astype(self.dtype)
        self.copy(3, t).start()
        self.copy(1, t).wait_recv()
        for i in (0, 1):
            self.zbuf[t, i, 2 * ab + a : 3 * ab] = (
                self.zbuf[t, i, 2 * ab + a : 3 * ab].astype(F32) + self.z_dn1[t, i, 0:b].astype(F32)
            ).astype(self.dtype)
        self.copy(4, t).start()
        self.copy(2, t).wait_recv()
        for z_to in range(4):
            first, second = self.places(xa, xb, z_to)
            both = (
                self.cbuf[t, 0, z_to].astype(F32) + self.c_in[t, z_to].astype(F32)
            ).astype(self.dtype)
            self.xz[t, self.at(first, xa)] = both[0:xa]
            self.xz[t, self.at(second, xb)] = both[xa:xr]
        self.copy(5, t).start()
        self.copy(6, t).start()

    def third(self, t):
        a, b, xa, xb = self.split
        ab, xr = a + b, xa + xb
        self.copy(3, t).wait_recv()
        self.copy(4, t).wait_recv()
        for i in (0, 1):
            place = jnp.where(self.x == i, 0, 1)
            self.fin[t, place, 0:a] = (
                self.zbuf[t, i, 3 * ab : 3 * ab + a].astype(F32)
                + self.z_up2[t, i].astype(F32)
                + self.z_dn1[t, i, b:ab].astype(F32)
            ).astype(self.dtype)
            self.fin[t, place, a:ab] = (
                self.zbuf[t, i, 3 * ab + a : 4 * ab].astype(F32)
                + self.z_dn2[t, i].astype(F32)
                + self.z_up1[t, i, a:ab].astype(F32)
            ).astype(self.dtype)
        self.copy(7, t).start()
        self.copy(5, t).wait_recv()
        self.xz[t, 2 * xr : 2 * xr + xa] = (
            self.xz[t, 2 * xr : 2 * xr + xa].astype(F32) + self.x_up1[t, 0:xa].astype(F32)
        ).astype(self.dtype)
        self.copy(8, t).start()
        self.copy(6, t).wait_recv()
        self.xz[t, 2 * xr + xa : 3 * xr] = (
            self.xz[t, 2 * xr + xa : 3 * xr].astype(F32) + self.x_dn1[t, 0:xb].astype(F32)
        ).astype(self.dtype)
        self.copy(9, t).start()

    def last(self, t):
        a, b, xa, xb = self.split
        ab, xr = a + b, xa + xb
        self.copy(7, t).wait_recv()
        one = self.fin[t, 0].astype(F32) + self.x_last[t].astype(F32)
        self.copy(8, t).wait_recv()
        self.copy(9, t).wait_recv()
        two = (
            self.xz[t, 3 * xr : 3 * xr + xa].astype(F32)
            + self.x_up2[t].astype(F32)
            + self.x_dn1[t, xb:xr].astype(F32)
        )
        three = (
            self.xz[t, 3 * xr + xa : 4 * xr].astype(F32)
            + self.x_dn2[t].astype(F32)
            + self.x_up1[t, xa:xr].astype(F32)
        )
        return one, two, three

    def finish(self):
        for k in range(MESSAGES):
            self.copy(k, slice(0, UNITS)).wait_send()


def kernel(
    x_hbm, gain_hbm, wq_hbm, wkv_hbm, wg_hbm, wu_hbm, k_hbm, v_hbm, len_ref,
    att_ref, hid,
    xbuf, gain, wq, wkv, wg, wu, keys, values, load_sem,
    piece, pbuf, ag_send, ag_recv, ag_side,
    qtmp, gtmp, utmp,
    qout, qin, q_send, q_recv,
    att1, att1_in, att1_send, att1_recv,
    att2, att2_in, att2_send, att2_recv,
    *sum_refs,
):
    w = lax.axis_index("wide")
    n = lax.axis_index("narrow")
    y, h, c = w // 4, lax.rem(w // 2, 2), lax.rem(w, 2)
    x, z = n // 4, lax.rem(n, 4)
    slab = piece.shape[3]
    tiles = slab // LANES
    rows = xbuf.shape[0]
    width = xbuf.shape[1]

    def wide(yy, hh, cc):
        return (yy * 2 + hh) * 2 + cc

    y_up = (wide(lax.rem(y + 1, 4), h, c), n)
    y_down = (wide(lax.rem(y + 3, 4), h, c), n)
    side = (wide(y, h, 1 - c), n)
    pair = (wide(y, 1 - h, c), (1 - x) * 4 + z)
    pair_up = (wide(lax.rem(y + 1, 4), 1 - h, c), (1 - x) * 4 + z)
    pair_down = (wide(lax.rem(y + 3, 4), 1 - h, c), (1 - x) * 4 + z)
    z_up = (w, x * 4 + lax.rem(z + 1, 4))
    z_down = (w, x * 4 + lax.rem(z + 3, 4))
    across = (w, (1 - x) * 4 + z)

    part = wg.shape[1] // PARTS
    pairs = [(x_hbm, xbuf), (gain_hbm, gain), (wq_hbm, wq), (wkv_hbm, wkv), (k_hbm, keys), (v_hbm, values)]
    for i in range(PARTS):
        cols = slice(i * part, (i + 1) * part)
        pairs += [(wg_hbm.at[:, cols], wg.at[:, cols]), (wu_hbm.at[:, cols], wu.at[:, cols])]
    loads = [pltpu.make_async_copy(src, dst, load_sem.at[i]) for i, (src, dst) in enumerate(pairs)]
    loads[0].start()

    barrier = pltpu.get_barrier_semaphore()
    for s in range(1, 16):
        pl.semaphore_signal(barrier, inc=1, device_id=(lax.rem(w + s, 16), n), device_id_type=MESH)
    for s in range(1, 8):
        pl.semaphore_signal(barrier, inc=1, device_id=(w, lax.rem(n + s, 8)), device_id_type=MESH)
    for other in (pair, pair_up, pair_down):
        pl.semaphore_signal(barrier, inc=1, device_id=other, device_id_type=MESH)

    for load in loads[1:4]:
        load.start()

    loads[0].wait()
    loads[1].wait()
    step_cols = 1024

    def add_block(i, total):
        block = xbuf[:, pl.ds(pl.multiple_of(i * step_cols, step_cols), step_cols)].astype(F32)
        for s in range(step_cols // 256):
            total = total + block[:, s * 256 : (s + 1) * 256]
        return total

    zero = jnp.zeros((rows, 256), F32)
    total = lax.fori_loop(0, width // step_cols, add_block, zero)
    average = jnp.sum(total, axis=1, keepdims=True) * (1.0 / width)

    def add_square(i, total):
        block = xbuf[:, pl.ds(pl.multiple_of(i * step_cols, step_cols), step_cols)].astype(F32)
        block = block - average
        block = block * block
        for s in range(step_cols // 256):
            total = total + block[:, s * 256 : (s + 1) * 256]
        return total

    total = lax.fori_loop(0, width // step_cols, add_square, zero)
    spread = jnp.sum(total, axis=1, keepdims=True) * (1.0 / width)
    factor = lax.rsqrt(spread + 1e-05)

    def normed(owner, i):
        start = pl.multiple_of(owner * slab + i * LANES, LANES)
        block = xbuf[:, pl.ds(start, LANES)].astype(F32)
        return ((block - average) * factor * gain[pl.ds(owner * tiles + i, 1), :]).astype(BF16)

    pair_n = (1 - x) * 4 + z
    for i in range(tiles):
        pbuf[:, i * LANES : (i + 1) * LANES] = normed(pair_n, i)
    for i in range(tiles):
        piece[0, c, :, i * LANES : (i + 1) * LANES] = normed(n, i)

    pl.semaphore_wait(barrier, 25)

    def gather_copy(k):
        src, slot, to = [
            (pbuf, 1, pair),
            (piece.at[0, c], 2, y_up),
            (piece.at[0, c], 3, y_down),
            (pbuf, 4, pair_up),
            (pbuf, 5, pair_down),
            (piece.at[2, c], 6, y_up),
            (piece.at[5, c], 7, y_down),
        ][k]
        return pltpu.make_async_remote_copy(
            src_ref=src, dst_ref=piece.at[slot, c], send_sem=ag_send.at[0], recv_sem=ag_recv.at[k],
            device_id=to, device_id_type=MESH,
        )

    def side_copy(t):
        return pltpu.make_async_remote_copy(
            src_ref=piece.at[t, c], dst_ref=piece.at[t, c], send_sem=ag_send.at[1],
            recv_sem=ag_side.at[t], device_id=side, device_id_type=MESH,
        )

    def side_wait(t):
        pltpu.make_async_remote_copy(
            src_ref=piece.at[t, 1 - c], dst_ref=piece.at[t, 1 - c], send_sem=ag_send.at[1],
            recv_sem=ag_side.at[t], device_id=side, device_id_type=MESH,
        ).wait_recv()

    side_copy(0).start()
    for k in (1, 2, 0, 3, 4):
        gather_copy(k).start()
    for load in loads[6:]:
        load.start()

    count = len(sum_refs) // 2
    q_sum = Summer(Q_SPLIT, F32, sum_refs[:count], (x, z), z_up, z_down, across)
    h_sum = Summer(H_SPLIT, BF16, sum_refs[count:], (x, z), z_up, z_down, across)

    def chip_of(t):
        group, odd = t // 2, lax.rem(t, 2)
        dy = jnp.where(group == 0, 0, jnp.where(group == 3, 2, jnp.where(odd == 0, 3, 1)))
        flip = jnp.where((group == 0) | (group == 3), odd, group - 1)
        return lax.rem(y + dy, 4), lax.rem(h + flip, 2)

    def project_q(t, count):
        size = count * 2 * rows
        for u in range(count):
            side_wait(t + u)
        block = piece[pl.ds(t, count)].reshape(size, slab)
        for s in range(3):
            qtmp[0:size, s * 256 : (s + 1) * 256] = jnp.dot(
                block, wq[:, s * 256 : (s + 1) * 256], preferred_element_type=F32
            )
        qtmp[0:size, 768:896] = jnp.zeros((size, LANES), F32)
        qtmp[0:size, 768:800] = lax.dot_general(
            block, wkv[...], (((1,), (1,)), ((), ())), preferred_element_type=F32
        )
        qtmp[0:size, 768:896] = pltpu.roll(qtmp[0:size, 768:896], 32 * lax.rem(w, 4), axis=1)

    def pack_q(t, base):
        low = lax.broadcasted_iota(jnp.int32, (8, 896), 0) < 4
        for m in range(4):
            top = qtmp[pl.ds(pl.multiple_of(base + 8 * m, 8), 8), :]
            bottom = qtmp[pl.ds(pl.multiple_of(base + rows + 8 * m, 8), 8), :]
            even = jnp.where(low, top, pltpu.roll(bottom, 4, axis=0))
            odd = jnp.where(low, pltpu.roll(top, 4, axis=0), bottom)
            for to, block in ((2 * m, even), (2 * m + 1, odd)):
                x_to, z_to = to // 4, to % 4
                first, second = q_sum.places(16, 16, z_to)
                far = jnp.where(x == x_to, 0, 1)
                for s in range(2):
                    q_sum.zbuf[t, x_to, q_sum.at(first + 8 * s, 8)] = block[:, s * 128 : (s + 1) * 128]
                    q_sum.zbuf[t, x_to, q_sum.at(second + 8 * s, 8)] = block[
                        :, (2 + s) * 128 : (3 + s) * 128
                    ]
                for s in range(3):
                    q_sum.cbuf[t, far, z_to, 8 * s : 8 * s + 8] = block[:, (4 + s) * 128 : (5 + s) * 128]
        q_sum.start_first(t)

    def pass_on(t):
        pltpu.make_async_remote_copy(
            src_ref=pbuf, dst_ref=piece.at[t, c], send_sem=ag_send.at[0],
            recv_sem=ag_recv.at[t - 1], device_id=side, device_id_type=MESH,
        ).wait_recv()
        side_copy(t).start()
        for slot, k in ((2, 5), (5, 6)):

            @pl.when(t == slot)
            def _():
                gather_copy(k).start()

    def project_h(t, count, first):
        size = count * 2 * rows
        block = piece[pl.ds(t, count)].reshape(size, slab)
        for s in range(gtmp.shape[1] // 256):
            if s * 256 % part == 0:

                @pl.when(first)
                def _():
                    loads[6 + 2 * (s * 256 // part)].wait()
                    loads[7 + 2 * (s * 256 // part)].wait()


            cols = slice(s * 256, (s + 1) * 256)
            gtmp[0:size, cols] = jnp.dot(block, wg[:, cols], preferred_element_type=F32).astype(BF16)
            utmp[0:size, cols] = jnp.dot(block, wu[:, cols], preferred_element_type=F32).astype(BF16)

    def pack_h(t, low):
        for to in range(8):
            x_to, z_to = to // 4, to % 4
            first, second = h_sum.places(80, 80, z_to)
            far = jnp.where(x == x_to, 0, 1)
            start = 288 * to
            base = start // LANES * LANES
            stop = min(-(-(start + 288) // LANES) * LANES, gtmp.shape[1])
            off = start - base
            g = gtmp[pl.ds(pl.multiple_of(low, 64), 2 * rows), base:stop]
            u = utmp[pl.ds(pl.multiple_of(low, 64), 2 * rows), base:stop]
            g0, g1, gr = g[:, off : off + 128], g[:, off + 128 : off + 256], g[:, off + 256 : off + 288]
            u0, u1, ur = u[:, off : off + 128], u[:, off + 128 : off + 256], u[:, off + 256 : off + 288]
            h_sum.zbuf[t, x_to, h_sum.at(first, 64)] = g0
            h_sum.zbuf[t, x_to, h_sum.at(first + 64, 16)] = g1[0:16]
            h_sum.zbuf[t, x_to, h_sum.at(second, 48)] = g1[16:64]
            h_sum.zbuf[t, x_to, h_sum.at(second + 48, 32)] = u0[0:32]
            h_sum.cbuf[t, far, z_to, 0:32] = u0[32:64]
            h_sum.cbuf[t, far, z_to, 32:96] = u1
            h_sum.cbuf[t, far, z_to, 96:128, 0:32] = gr[0:32]
            h_sum.cbuf[t, far, z_to, 96:128, 32:64] = ur[0:32]
            h_sum.cbuf[t, far, z_to, 96:128, 64:96] = gr[32:64]
            h_sum.cbuf[t, far, z_to, 96:128, 96:128] = ur[32:64]
        h_sum.start_first(t)

    def q_copy(t, core):
        yy, hh = chip_of(t)
        to = wide(yy, hh, core)
        return to, pltpu.make_async_remote_copy(
            src_ref=qout.at[t, core], dst_ref=qin.at[w], send_sem=q_send.at[0],
            recv_sem=q_recv.at[0], device_id=(to, n), device_id_type=MESH,
        )

    def finish_q(t):
        one, two, three = q_sum.last(t)
        blocks = [one[8 * s : 8 * s + 8] for s in range(4)]
        blocks += [two[0:8], two[8:16], three]
        blocks = [block.astype(BF16).astype(F32) for block in blocks]
        for core in range(2):
            for s, block in enumerate(blocks):
                qout[t, core, :, s * 128 : (s + 1) * 128] = block[4 * core : 4 * core + 4]
            to, copy = q_copy(t, core)

            @pl.when(to != w)
            def _():
                copy.start()

            @pl.when(to == w)
            def _():
                for s, block in enumerate(blocks):
                    qin[w, :, s * 128 : (s + 1) * 128] = block[4 * core : 4 * core + 4]

    def silu(v):
        return v / (1.0 + jnp.exp(-v))

    def finish_h(t):
        one, two, three = h_sum.last(t)
        yy, hh = chip_of(t)
        start = (yy * 2 + hh) * 64

        def out_rows(offset, size):
            return pl.ds(pl.multiple_of(start + offset, 32), size)

        hid[out_rows(0, 32), 0:128] = (silu(one[0:32]) * one[128:160]).astype(BF16)
        hid[out_rows(32, 32), 0:128] = (silu(one[32:64]) * two[0:32]).astype(BF16)
        hid[out_rows(0, 32), 128:256] = (silu(one[64:96]) * two[32:64]).astype(BF16)
        hid[out_rows(32, 32), 128:256] = (silu(one[96:128]) * three[0:32]).astype(BF16)
        rest = three[32:64]
        rest = silu(rest) * pltpu.roll(rest, 96, axis=1)
        hid[out_rows(0, 32), 256:288] = rest[:, 0:32].astype(BF16)
        hid[out_rows(32, 32), 256:288] = pltpu.roll(rest, 64, axis=1)[:, 0:32].astype(BF16)

    def wait_all(buffer, send, recv):
        part = buffer.at[0 : buffer.shape[0] - 1]
        return pltpu.make_async_remote_copy(
            src_ref=part, dst_ref=part, send_sem=send.at[0], recv_sem=recv.at[0],
            device_id=side, device_id_type=MESH,
        )

    def att1_copy(s):
        to = lax.rem(n + s, 8)
        return pltpu.make_async_remote_copy(
            src_ref=att1.at[to], dst_ref=att1_in.at[n], send_sem=att1_send.at[0],
            recv_sem=att1_recv.at[0], device_id=(w, to), device_id_type=MESH,
        )

    def att2_copy(s):
        to = lax.rem(w + s, 16)
        return pltpu.make_async_remote_copy(
            src_ref=att2.at[to], dst_ref=att2_in.at[w], send_sem=att2_send.at[0],
            recv_sem=att2_recv.at[0], device_id=(to, n), device_id_type=MESH,
        )

    def attend():
        loads[4].wait()
        loads[5].wait()

        wait_all(qin, q_send, q_recv).wait_recv()

        scale = 256 ** (-0.5)
        for r in range(4):
            heads = jnp.concatenate(
                [qin[:, r, s * 256 : (s + 1) * 256] for s in range(3)], axis=0
            )
            kv = qin[:, r, 768:896]
            kv = [jnp.sum(kv[4 * i : 4 * i + 4], axis=0, keepdims=True) for i in range(4)]
            own_key = jnp.concatenate(kv[0:2], axis=1)
            own_value = jnp.concatenate(kv[2:4], axis=1)
            scores = lax.dot_general(
                heads.astype(BF16), keys[r], (((1,), (1,)), ((), ())), preferred_element_type=F32
            ) * scale
            valid = lax.broadcasted_iota(jnp.int32, scores.shape, 1) < len_ref[r]
            raised = jnp.where(valid, jnp.exp(scores), 0.0)
            own = jnp.exp(jnp.sum(heads * own_key, axis=1, keepdims=True) * scale)
            total = jnp.sum(raised, axis=1, keepdims=True) + own
            probs = (raised / total).astype(BF16)
            own_prob = (own / total).astype(BF16).astype(F32)
            out = jnp.dot(probs, values[r], preferred_element_type=F32) + own_prob * own_value
            flat = jnp.concatenate(
                [out[0:16], out[16:32], out[32:48], jnp.zeros((16, LANES), F32)], axis=1
            )
            for to in range(8):
                att1[to, r] = flat[:, 96 * to : 96 * to + 128].astype(BF16)
        att1_in[n] = att1[n]
        for s in range(1, 8):
            att1_copy(s).start()

    def spread_heads():
        wait_all(att1_in, att1_send, att1_recv).wait_recv()
        att2[...] = jnp.swapaxes(att1_in[...].reshape(32, 16, LANES), 0, 1)
        att2_in[w] = att2[w]
        for s in range(1, 16):
            att2_copy(s).start()

    def gather_heads():
        wait_all(att2_in, att2_send, att2_recv).wait_recv()
        att_ref[...] = att2_in[...].reshape(512, LANES)

    def look_up(i, table):
        start, count = jnp.int32(0), jnp.int32(0)
        for at, (first, size) in table.items():
            start = jnp.where(i == at, first, start)
            count = jnp.where(i == at, size, count)
        return start, count

    def run(i, table, step):
        start, count = look_up(i, table)

        @pl.loop(0, count)
        def _(u):
            step(start + u)

    def project(i, table, step, pack, *more):
        start, count = look_up(i, table)
        for size in sorted({size for _, size in table.values()}):

            @pl.when(count == size)
            def _():
                step(start, size, *more)

        @pl.loop(0, count)
        def _(u):
            pack(start + u, u * 2 * rows)

    first_h = min(H_PROJECT)
    loads[2].wait()
    loads[3].wait()

    @pl.loop(0, PASSES)
    def _(i):
        run(i, GATHER, pass_on)
        project(i, Q_PROJECT, project_q, pack_q)
        project(i, H_PROJECT, project_h, pack_h, i == first_h)

        @pl.when(i == first_h)
        def _():
            loads[4].start()
            loads[5].start()

        run(i, Q_SECOND, q_sum.second)
        run(i, Q_THIRD, q_sum.third)
        run(i, H_SECOND, h_sum.second)
        run(i, H_THIRD, h_sum.third)
        run(i, Q_LAST, finish_q)
        run(i, H_LAST, finish_h)

        @pl.when(i == ATTEND)
        def _():
            attend()

        @pl.when(i == SPREAD)
        def _():
            spread_heads()

    gather_heads()

    for part, sem in ((piece.at[0:7, 0], 0), (piece.at[:, 0], 1)):
        pltpu.make_async_remote_copy(
            src_ref=part, dst_ref=part, send_sem=ag_send.at[sem], recv_sem=ag_recv.at[0],
            device_id=side, device_id_type=MESH,
        ).wait_send()
    q_sum.finish()
    h_sum.finish()
    wait_all(qin, q_send, q_recv).wait_send()
    wait_all(att1_in, att1_send, att1_recv).wait_send()
    wait_all(att2_in, att2_send, att2_recv).wait_send()


def turn(att, hid, att_out, hid_out):
    for i in range(4):
        cols = slice(i * 128, (i + 1) * 128)
        att_out[:, cols] = att[cols, :].T[0:96]
        hid_out[0:128, cols] = hid[cols, 0:128].T
        hid_out[128:256, cols] = hid[cols, 128:256].T
        hid_out[256:288, cols] = hid[cols, 256:384].T[0:32]


def body(
    layer_input, norm_gain, w_query, w_keyvalue, w_gate, w_up, key_cache, value_cache, cache_lengths
):
    rows, width = layer_input.shape
    slab = w_query.shape[0]
    anywhere = pl.BlockSpec(memory_space=pl.ANY)
    vmem = pl.BlockSpec(memory_space=pltpu.VMEM)
    dma = pltpu.SemaphoreType.DMA
    attended, hidden = pl.pallas_call(
        kernel,
        out_shape=(
            jax.ShapeDtypeStruct((512, LANES), BF16),
            jax.ShapeDtypeStruct((512, 3 * LANES), BF16),
        ),
        in_specs=[anywhere] * 8 + [pl.BlockSpec(memory_space=pltpu.SMEM)],
        out_specs=(vmem, vmem),
        scratch_shapes=[
            pltpu.VMEM((rows, width), BF16),
            pltpu.VMEM((width // LANES, LANES), F32),
            pltpu.VMEM(w_query.shape, BF16),
            pltpu.VMEM(w_keyvalue.shape[::-1], BF16),
            pltpu.VMEM(w_gate.shape, BF16),
            pltpu.VMEM(w_up.shape, BF16),
            pltpu.VMEM(key_cache.shape, BF16),
            pltpu.VMEM(value_cache.shape, BF16),
            dma((6 + 2 * PARTS,)),
            pltpu.VMEM((UNITS, 2, rows, slab), BF16),
            pltpu.VMEM((rows, slab), BF16),
            dma((2,)),
            dma((7,)),
            dma((8,)),
            pltpu.VMEM((4 * rows, 896), F32),
            pltpu.VMEM((4 * rows, w_gate.shape[1]), BF16),
            pltpu.VMEM((4 * rows, w_up.shape[1]), BF16),
            pltpu.VMEM((UNITS, 2, 4, 896), F32),
            pltpu.VMEM((16, 4, 896), F32),
            dma((1,)),
            dma((1,)),
            pltpu.VMEM((8, 4, 16, LANES), BF16),
            pltpu.VMEM((8, 4, 16, LANES), BF16),
            dma((1,)),
            dma((1,)),
            pltpu.VMEM((16, 32, LANES), BF16),
            pltpu.VMEM((16, 32, LANES), BF16),
            dma((1,)),
            dma((1,)),
        ]
        + sum_scratch(Q_SPLIT, F32)
        + sum_scratch(H_SPLIT, BF16),
        compiler_params=pltpu.CompilerParams(
            collective_id=0, has_side_effects=True, vmem_limit_bytes=60 * 1024 * 1024
        ),
    )(
        layer_input, norm_gain.reshape(width // LANES, LANES), w_query, w_keyvalue.T, w_gate, w_up,
        key_cache, value_cache, cache_lengths,
    )
    attended, hidden = pl.pallas_call(
        turn,
        out_shape=(
            jax.ShapeDtypeStruct((96, 512), BF16),
            jax.ShapeDtypeStruct((288, 512), BF16),
        ),
        in_specs=[vmem, vmem],
        out_specs=(vmem, vmem),
    )(attended, hidden)
    return attended.T, hidden.T


def solution(mesh):
    placed = (
        P("wide", None),
        P(),
        P("narrow", "wide"),
        P("narrow", "wide"),
        P("narrow", "wide"),
        P("narrow", "wide"),
        P(("wide", "narrow"), None, None),
        P(("wide", "narrow"), None, None),
        P(("wide", "narrow")),
    )
    return jax.shard_map(
        body,
        mesh=mesh,
        in_specs=placed,
        out_specs=(P(None, ("wide", "narrow")), P(None, ("wide", "narrow"))),
        check_vma=False,
    )
```
